32 devices in a mesh: dp: 8 (over z, y), tensor: 4 (over x, core).
Axes of the slice: x: 2, y: 2, z: 4, core: 2. Of those that a mesh axis runs over, the one named last changes fastest.
Arguments:
- tokens: bfloat16 [16, 1024, 1536], P('dp', 'tensor'), may hold values from -6 to 6
- context: bfloat16 [16, 130, 768], P('dp'), may hold values from -6 to 6
- positions: int32 [16, 1024], P('dp'), may hold values from 0 to 4095
- seq_mask: int32 [16], P('dp'), may hold values 0 or 1
- cotangent: bfloat16 [16, 1024, 1536], P('dp', 'tensor'), may hold values from -6 to 6
- norm_gains: float32 [3, 1536], P(None, ('dp', 'tensor')), may hold values from 0.25 to 1.75
- norm_shifts: float32 [3, 1536], P(None, ('dp', 'tensor')), may hold values from -3 to 3
- w_qkv: bfloat16 [3, 1536, 1536], P(None, 'dp', 'tensor'), may hold values from -0.15625 to 0.15625
- w_self_out: bfloat16 [1536, 1536], P('tensor', 'dp'), may hold values from -2.5 to 2.5
- w_cross_q: bfloat16 [1536, 1536], P('dp', 'tensor'), may hold values from -0.15625 to 0.15625
- w_cross_kv: bfloat16 [2, 768, 1536], P(None, 'dp', 'tensor'), may hold values from -0.21875 to 0.21875
- w_cross_out: bfloat16 [1536, 1536], P('tensor', 'dp'), may hold values from -0.875 to 0.875
- w_gate_up: bfloat16 [2, 1536, 6144], P(None, 'dp', 'tensor'), may hold values from -0.15625 to 0.15625
- w_down: bfloat16 [6144, 1536], P('tensor', 'dp'), may hold values from -0.15625 to 0.15625
Outputs:
- out: bfloat16 [16, 1024, 1536], P('dp', 'tensor')
- grad_input: float32 [16, 1024, 1536], P('dp', 'tensor')
- grad_norm_gains: float32 [3, 1536], P(None, ('dp', 'tensor'))
- grad_norm_shifts: float32 [3, 1536], P(None, ('dp', 'tensor'))
- grad_qkv: float32 [3, 1536, 1536], P(None, 'dp', 'tensor')
- grad_self_out: float32 [1536, 1536], P('tensor', 'dp')
- grad_cross_q: float32 [1536, 1536], P('dp', 'tensor')
- grad_cross_kv: float32 [2, 768, 1536], P(None, 'dp', 'tensor')
- grad_cross_out: float32 [1536, 1536], P('tensor', 'dp')
- grad_gate_up: float32 [2, 1536, 6144], P(None, 'dp', 'tensor')
- grad_down: float32 [6144, 1536], P('tensor', 'dp')
The draws below stay inside these ranges and needn't reach their ends.
Inputs may be any that keep to these rules, and one draw needn't show every extreme that they name: `seq_mask`: 1 marks a sequence slot that holds data, 0 an empty slot.
All inputs are finite; a program needn't handle non-finite values. No bound on the sum of `seq_mask` on one device may be relied on, other than what follows from the above.
Results may differ from the reference program's by a relative error of at most 0.02.
Values may be sent and summed in bfloat16 or wider, within the bound.
No kernel may reach another device: no remote copies, remote signals or barrier semaphores. Data moves between devices by JAX's collectives and lax.ppermute only.
A program may use at most 256 MiB of HBM per device.

```python
import math
import jax
import jax.numpy as jnp
from jax import lax

D = 1536
HEADS = 24
HEAD_WIDTH = 64
FF = 6144
CD = 768
CTX = 130
ROT = 32
LEN = 1024
SEQS = 16


def set_ends(values, key, least, high):
    extent = values.shape
    place = [jax.random.randint(jax.random.fold_in(key, axis), (), 0, extent[axis]) for axis in range(len(extent))]
    values = values.at[tuple(place)].set(least)
    longest = extent.index(max(extent))
    place[longest] = (place[longest] + 1) % extent[longest]
    return values.at[tuple(place)].set(high)


def shard_levels(stream_key, shape, pieces, low, largest):
    def one(position, shards_of):
        heights = jax.random.uniform(jax.random.fold_in(jax.random.fold_in(stream_key, 6), position), (shards_of,), jnp.float32, low / len(pieces), largest / len(pieces))
        return jnp.repeat(jnp.exp(heights), shape[position] // shards_of).reshape((-1,) + (1,) * (len(shape) - position - 1))

    loudness = one(*pieces[0])
    for cut in pieces[1:]:
        loudness = loudness * one(*cut)
    return loudness


def noise(rng, dims, scale, reach, pieces=(), kind=jnp.bfloat16):
    values = jax.random.normal(rng, dims, jnp.float32) * scale
    if len(pieces) > 0:
        values = shard_levels(rng, dims, pieces, -0.22, 0.18) * values
    return jnp.clip(values, min=-reach, max=reach).astype(kind)


def setup_inputs(seed: int = 0) -> dict:
    key_list = jax.random.split(jax.random.key(seed), 15)
    tokens = noise(key_list[0], (SEQS, LEN, D), 1.0, 6.0, ((0, 8), (1, 4)))
    context = noise(key_list[1], (SEQS, CTX, CD), 1.0, 6.0, ((0, 8),))
    positions = set_ends(jax.random.randint(key_list[2], (SEQS, LEN), 0, 4096), jax.random.fold_in(key_list[2], 1), 0, 4095).astype(jnp.int32)
    seq_mask = set_ends((jax.random.randint(key_list[3], (SEQS,), 0, 64) < 47).astype(jnp.int32), jax.random.fold_in(key_list[3], 1), 0, 1)
    cotangent = noise(key_list[4], (SEQS, LEN, D), 1.0, 6.0, ((0, 8), (1, 4)))
    norm_gains = jnp.clip(1.0 + 0.15 * jax.random.normal(key_list[5], (3, D), jnp.float32), 0.25, 1.75)
    norm_shifts = noise(key_list[6], (3, D), 0.5, 3.0, ((1, 32),), jnp.float32)
    w_qkv = noise(key_list[7], (3, D, HEADS * HEAD_WIDTH), D ** -0.5, 0.15625, ((1, 8), (2, 4)))
    w_self_out = noise(key_list[8], (HEADS * HEAD_WIDTH, D), (HEADS * HEAD_WIDTH * 4 // LEN) ** -0.5, 2.5, ((0, 4), (1, 8)))
    w_cross_q = noise(key_list[9], (D, HEADS * HEAD_WIDTH), D ** -0.5, 0.15625, ((0, 8), (1, 4)))
    w_cross_kv = noise(key_list[10], (2, CD, HEADS * HEAD_WIDTH), CD ** -0.5, 0.21875, ((1, 8), (2, 4)))
    w_cross_out = noise(key_list[11], (HEADS * HEAD_WIDTH, D), (HEADS * HEAD_WIDTH * 4 // CTX) ** -0.5, 0.875, ((0, 4), (1, 8)))
    w_gate_up = noise(key_list[12], (2, D, FF), D ** -0.5, 0.15625, ((1, 8), (2, 4)))
    w_down = noise(key_list[13], (FF, D), (FF // 4) ** -0.5, 0.15625, ((0, 4), (1, 8)))
    return dict(tokens=tokens, context=context, positions=positions, seq_mask=seq_mask, cotangent=cotangent, norm_gains=norm_gains, norm_shifts=norm_shifts, w_qkv=w_qkv, w_self_out=w_self_out, w_cross_q=w_cross_q, w_cross_kv=w_cross_kv, w_cross_out=w_cross_out, w_gate_up=w_gate_up, w_down=w_down)


EPS = 1e-05
EXACT_ARITHMETIC = lax.Precision.HIGHEST

@jax.custom_vjp
def low(v):
    return lax.optimization_barrier(v.astype(jnp.bfloat16)).astype(jnp.float32)

@jax.custom_vjp
def reduced_pullback(v):
    return v

def low_keep(v):
    return (low(v), None)

def low_pass(kept, grad):
    return (grad,)

def back_keep(v):
    return (v, None)

def back_low(kept, grad):
    return (low(grad),)
low.defvjp(low_keep, low_pass)
reduced_pullback.defvjp(back_keep, back_low)

def product(left_side, right_side):
    return jnp.dot(left_side, right_side, precision=EXACT_ARITHMETIC)

def tables(pos_row):
    half_rot = ROT // 2
    inverse = jnp.exp(jnp.arange(half_rot, dtype=jnp.float32) * (-2.0 * math.log(10000.0) / ROT))
    angles = pos_row.astype(jnp.float32)[:, None] * inverse[None, :]
    return (jnp.cos(angles), jnp.sin(angles))

def rotate(input_values, cosine, sine_table):
    half_rot = cosine.shape[-1]
    first_half = input_values[..., :half_rot]
    second_half = input_values[..., half_rot:2 * half_rot]
    rest_dims = input_values[..., 2 * half_rot:]
    cos_b = cosine[:, None, :]
    sin_b = sine_table[:, None, :]
    return jnp.concatenate([first_half * cos_b - second_half * sin_b, second_half * cos_b + first_half * sin_b, rest_dims], axis=-1)

def layer_normalize(token_rows, gain_row, shift_row):
    mean_row = lax.optimization_barrier(jnp.mean(token_rows, axis=-1, keepdims=True))
    centred = token_rows - mean_row
    variance = lax.optimization_barrier(jnp.mean(centred * centred, axis=-1, keepdims=True))
    return centred * lax.rsqrt(variance + EPS) * gain_row + shift_row

def attend(queries, input_keys, input_values):
    length = queries.shape[0]
    block_rows = min(512, length)
    blocks = queries.reshape(length // block_rows, block_rows, queries.shape[1], queries.shape[2])

    def per_block(query_block):
        attention_logits = reduced_pullback(jnp.einsum('ioc,soc->ois', query_block, input_keys, precision=EXACT_ARITHMETIC) * HEAD_WIDTH ** (-0.5))
        reduced_weights = low(jax.nn.softmax(attention_logits, axis=-1))
        return jnp.einsum('roe,erg->org', reduced_weights, input_values, precision=EXACT_ARITHMETIC)
    result = lax.map(jax.checkpoint(per_block), blocks)
    return result.reshape(length, queries.shape[1] * queries.shape[2])

def layer_one(params, token_rows, cond_rows, pos_row, keep_scale):
    norm_gains, norm_shifts, w_qkv, w_self_out, w_cross_q, w_cross_kv, w_cross_out, w_gate_up, w_down = params
    length = token_rows.shape[0]
    ctx_len = cond_rows.shape[0]
    cosine, sine_table = tables(pos_row)
    normed = low(layer_normalize(token_rows, norm_gains[0], norm_shifts[0]))
    q_pre = reduced_pullback(product(normed, w_qkv[0])).reshape(length, HEADS, HEAD_WIDTH)
    k_pre = reduced_pullback(product(normed, w_qkv[1])).reshape(length, HEADS, HEAD_WIDTH)
    v_pre = reduced_pullback(product(normed, w_qkv[2])).reshape(length, HEADS, HEAD_WIDTH)
    queries = low(rotate(q_pre, cosine, sine_table))
    keys_rot = low(rotate(k_pre, cosine, sine_table))
    values_low = low(v_pre)
    attended = low(reduced_pullback(attend(queries, keys_rot, values_low)))
    leading_sum = token_rows + reduced_pullback(product(attended, w_self_out))
    normed = low(layer_normalize(leading_sum, norm_gains[1], norm_shifts[1]))
    cross_q = low(reduced_pullback(product(normed, w_cross_q))).reshape(length, HEADS, HEAD_WIDTH)
    cross_k = low(reduced_pullback(product(cond_rows, w_cross_kv[0]))).reshape(ctx_len, HEADS, HEAD_WIDTH)
    cross_v = low(reduced_pullback(product(cond_rows, w_cross_kv[1]))).reshape(ctx_len, HEADS, HEAD_WIDTH)
    crossed = low(reduced_pullback(attend(cross_q, cross_k, cross_v)))
    trailing_sum = leading_sum + reduced_pullback(product(crossed, w_cross_out))
    normed = low(layer_normalize(trailing_sum, norm_gains[2], norm_shifts[2]))
    gate_pre = reduced_pullback(product(normed, w_gate_up[0]))
    up_pre = reduced_pullback(product(normed, w_gate_up[1]))
    hidden = low(jax.nn.silu(gate_pre) * up_pre)
    third_sum = trailing_sum + reduced_pullback(product(hidden, w_down))
    return third_sum * keep_scale

def reference(tokens, context, positions, seq_mask, cotangent, norm_gains, norm_shifts, w_qkv, w_self_out, w_cross_q, w_cross_kv, w_cross_out, w_gate_up, w_down):
    context_f = context.astype(jnp.float32)
    keep_all = seq_mask.astype(jnp.float32)
    params = (norm_gains.astype(jnp.float32), norm_shifts.astype(jnp.float32), w_qkv.astype(jnp.float32), w_self_out.astype(jnp.float32), w_cross_q.astype(jnp.float32), w_cross_kv.astype(jnp.float32), w_cross_out.astype(jnp.float32), w_gate_up.astype(jnp.float32), w_down.astype(jnp.float32))

    def forward(param_set, tok_all):
        stepper = jax.checkpoint(layer_one)

        def per_item(item_args):
            return stepper(param_set, item_args[0], item_args[1], item_args[2], item_args[3])
        return lax.map(per_item, (tok_all, context_f, positions, keep_all))
    result, pull_back = jax.vjp(forward, params, tokens.astype(jnp.float32))
    grad_params, grad_tokens = pull_back(cotangent.astype(jnp.float32))
    return (result.astype(jnp.bfloat16), grad_tokens, grad_params[0], grad_params[1], grad_params[2], grad_params[3], grad_params[4], grad_params[5], grad_params[6], grad_params[7], grad_params[8])
```

```python
import functools
import math

import jax
import jax.numpy as jnp
from jax import lax
from jax.experimental import pallas as pl
from jax.experimental.pallas import tpu as pltpu
from jax.sharding import PartitionSpec as P

HEAD_WIDTH = 64
ROT = 32
EPS = 1e-05
BF = jnp.bfloat16
F32 = jnp.float32
LOG2E = math.log2(math.e)
VMEM_BYTES = 56 * 1024 * 1024


def call(kernel, outs, grid, in_specs, out_specs, scratch, flops, moved, operands):
    return pl.pallas_call(
        kernel,
        out_shape=outs,
        grid=grid,
        in_specs=in_specs,
        out_specs=out_specs,
        scratch_shapes=scratch,
        compiler_params=pltpu.CompilerParams(vmem_limit_bytes=VMEM_BYTES),
        cost_estimate=pl.CostEstimate(flops=flops, bytes_accessed=moved, transcendentals=0),
    )(*operands)


def shape(dims, kind=BF):
    return jax.ShapeDtypeStruct(dims, kind)


def whole(dims):
    return pl.BlockSpec(dims, lambda *_: (0,) * len(dims))


SMEM = pl.BlockSpec(memory_space=pltpu.SMEM)


def dot_nn(a, b):
    return jnp.dot(a, b, preferred_element_type=F32)


def dot_nt(a, b):
    return lax.dot_general(a, b, (((1,), (1,)), ((), ())), preferred_element_type=F32)


def dot_tn(a, b):
    return lax.dot_general(a, b, (((0,), (0,)), ((), ())), preferred_element_type=F32)


def assemble(parity, own, other, scratch):
    pairs, _, rows, width = scratch.shape
    scratch[:, pl.ds(parity, 1)] = own[...].reshape(pairs, 1, rows, width)
    scratch[:, pl.ds(1 - parity, 1)] = other[...].reshape(pairs, 1, rows, width)
    return scratch[...].reshape(pairs * 2 * rows, width)


def split_rows(parity, value, scratch, own, other, columns):
    pairs, _, rows, width = scratch.shape
    scratch[...] = value.reshape(scratch.shape)
    own[:, columns] = scratch[:, pl.ds(parity, 1)].reshape(pairs * rows, width)
    other[:, columns] = scratch[:, pl.ds(1 - parity, 1)].reshape(pairs * rows, width)


def rope(v, cosine, low_sine, high_sine, sign):
    width = v.shape[-1]
    half = ROT // 2
    ahead = pltpu.roll(v, width - half, 1)
    behind = pltpu.roll(v, half, 1)
    return v * cosine + sign * (behind * high_sine - ahead * low_sine)


def head_mask(h):
    lane = lax.broadcasted_iota(jnp.int32, (1, 2 * HEAD_WIDTH), 1)
    return (lane // HEAD_WIDTH) == h


def attend_rows(q_ref, k_ref, v_ref, att_ref, lse_scratch, valid):
    length, width = q_ref.shape
    keys = k_ref.shape[0]
    block = min(256, length)
    scale = HEAD_WIDTH**-0.5 * LOG2E
    lanes = 2 * HEAD_WIDTH

    def rows_step(i, _):
        rows = pl.ds(pl.multiple_of(i * block, block), block)
        lane = lax.broadcasted_iota(jnp.int32, (block, lanes), 1)
        sums = jnp.zeros((block, lanes), F32)
        for pair in range(width // lanes):
            columns = slice(pair * lanes, (pair + 1) * lanes)
            q = q_ref[rows, columns]
            total = None
            for h in range(2):
                mask = head_mask(h)
                k = jnp.where(mask, k_ref[:, columns], jnp.zeros((), BF))
                v = jnp.where(mask, v_ref[:, columns], jnp.zeros((), BF))
                logits = dot_nt(q, k) * scale
                if valid < keys:
                    spot = lax.broadcasted_iota(jnp.int32, logits.shape, 1)
                    logits = jnp.where(spot < valid, logits, -jnp.inf)
                peak = jnp.max(logits, axis=1, keepdims=True)
                weights = jnp.exp2(logits - peak)
                norm = jnp.sum(weights, axis=1, keepdims=True)
                term = dot_nn(weights.astype(BF), v) / norm
                total = term if total is None else total + term
                sums = jnp.where(lane == pair * 2 + h, peak + jnp.log2(norm), sums)
            att_ref[rows, columns] = total.astype(BF)
        lse_scratch[rows, :] = sums
        return 0

    lax.fori_loop(0, length // block, rows_step, 0)


def attend_back(q_ref, k_ref, v_ref, att_ref, do_ref, lse_ref, dq_acc, put_k, put_v, put_q, valid):
    length, width = q_ref.shape
    keys = k_ref.shape[0]
    block = min(256, keys)
    scale = HEAD_WIDTH**-0.5
    lanes = 2 * HEAD_WIDTH
    for pair in range(width // lanes):
        columns = slice(pair * lanes, (pair + 1) * lanes)
        product = do_ref[:, columns].astype(F32) * att_ref[:, columns].astype(F32)
        deltas = []
        for h in range(2):
            ones = jnp.where(head_mask(h), 1.0, 0.0).astype(F32)
            deltas.append(
                lax.dot_general(
                    jnp.broadcast_to(ones, (8, lanes)),
                    product,
                    (((1,), (1,)), ((), ())),
                    preferred_element_type=F32,
                    precision=lax.Precision.HIGHEST,
                )[:1]
            )
        dq_acc[...] = jnp.zeros_like(dq_acc)

        def keys_step(i, _):
            rows = pl.ds(pl.multiple_of(i * block, block), block)
            dk_total, dv_total = None, None
            for h in range(2):
                mask = head_mask(h)
                zero = jnp.zeros((), BF)
                k = jnp.where(mask, k_ref[rows, columns], zero)
                v = jnp.where(mask, v_ref[rows, columns], zero)
                q = q_ref[:, columns]
                do = do_ref[:, columns]
                head = pair * 2 + h
                logits = dot_nt(k, q) * (scale * LOG2E)
                weights = jnp.exp2(logits - lse_ref[head : head + 1, :])
                if valid < keys:
                    spot = i * block + lax.broadcasted_iota(jnp.int32, weights.shape, 0)
                    weights = jnp.where(spot < valid, weights, 0.0)
                dp = dot_nt(v, do)
                ds = (weights * (dp - deltas[h])).astype(BF)
                dv = dot_nn(weights.astype(BF), jnp.where(mask, do, zero))
                dk = dot_nn(ds, jnp.where(mask, q, zero))
                dq_acc[...] += dot_tn(ds, k)
                dk_total = dk if dk_total is None else dk_total + dk
                dv_total = dv if dv_total is None else dv_total + dv
            put_k(rows, columns, dk_total * scale)
            put_v(rows, columns, dv_total)
            return 0

        lax.fori_loop(0, keys // block, keys_step, 0)
        put_q(columns, dq_acc[...] * scale)


def finish_sums(lse_scratch, lse_ref):
    lse_ref[...] = jnp.transpose(lse_scratch[...])[: lse_ref.shape[0]]


def row_norm(t):
    mean = jnp.mean(t, axis=-1, keepdims=True)
    centred = t - mean
    return centred * lax.rsqrt(jnp.mean(centred * centred, axis=-1, keepdims=True) + EPS)


def self_forward(parity, parts, seq, gain, shift, w_own, w_other, cos, low, high, heads):
    part_rows, model = parts[0].shape[1:]
    length = part_rows * len(parts)
    width = heads * HEAD_WIDTH
    lanes = 2 * HEAD_WIDTH
    pairs_rows = w_own.shape[0]

    def kernel(par, p0, p1, p2, p3, g, b, own, other, c_ref, l_ref, h_ref, normed, q, k, v, att, lse, scr, sums):
        for i, part in enumerate((p0, p1, p2, p3)):
            rows = slice(i * part_rows, (i + 1) * part_rows)
            normed[rows, :] = (row_norm(part[0].astype(F32)) * g[...] + b[...]).astype(BF)
        weight = assemble(par[0], own, other, scr)
        for j, target in enumerate((q, k, v)):
            value = dot_nn(normed[...], weight[:, j * width : (j + 1) * width])
            if j == 2:
                target[...] = value.astype(BF)
                continue
            for pair in range(width // lanes):
                columns = slice(pair * lanes, (pair + 1) * lanes)
                target[:, columns] = rope(value[:, columns], c_ref[...], l_ref[...], h_ref[...], 1.0).astype(BF)
        attend_rows(q, k, v, att, sums, length)
        finish_sums(sums, lse)

    part_spec = pl.BlockSpec((1, part_rows, model), lambda *_: (seq, 0, 0))
    table_spec = whole((length, lanes))
    dp = 2 * (pairs_rows // 1)
    return call(
        kernel,
        (shape((length, model)),) + (shape((length, width)),) * 4 + (shape((8, length), F32),),
        (1,),
        [SMEM] + [part_spec] * 4 + [whole((1, model))] * 2 + [whole(w_own.shape)] * 2 + [table_spec] * 3,
        (whole((length, model)),) + (whole((length, width)),) * 4 + (whole((8, length)),),
        [pltpu.VMEM(scratch_dims(model, w_own), BF), pltpu.VMEM((length, lanes), F32)],
        2 * length * model * 3 * width + 4 * length * length * width,
        16_000_000,
        (parity, *parts, gain, shift, w_own, w_other, cos, low, high),
    )


PAIRS = {}


def scratch_dims(model, w_own):
    pairs = PAIRS["pairs"]
    return (pairs, 2, w_own.shape[0] // pairs, w_own.shape[1])


def project(parity, rows, w_own, w_other, column, model):
    length, width = rows.shape
    half_rows = length // 2
    pairs = PAIRS["pairs"]
    w_rows = w_own.shape[0]

    def kernel(par, a, own, other, keep, send, scr):
        weight = assemble(par[0], own, other, scr)
        send[...] = dot_nt(a[half_rows:, :], weight).astype(BF)
        keep[...] = dot_nt(a[:half_rows, :], weight).astype(BF)

    w_spec = pl.BlockSpec((w_rows, width), lambda *_: (0, column))
    return call(
        kernel,
        (shape((half_rows, model)),) * 2,
        (1,),
        [SMEM, whole((length, width)), w_spec, w_spec],
        (whole((half_rows, model)),) * 2,
        [pltpu.VMEM((pairs, 2, w_rows // pairs, width), BF)],
        2 * length * width * model,
        length * (width + model) * 2 + 2 * w_rows * width * 2,
        (parity, rows, w_own, w_other),
    )


def cross_forward(parity, parts, w_own, w_other, column, keys, values, valid):
    part_rows, model = parts[0].shape
    length = part_rows * len(parts)
    width = keys.shape[1]
    count = keys.shape[0]
    lanes = 2 * HEAD_WIDTH
    pairs = PAIRS["pairs"]
    w_rows = w_own.shape[0]

    def kernel(par, p0, p1, p2, p3, own, other, k, v, q, att, lse, scr, sums):
        weight = assemble(par[0], own, other, scr)
        for i, part in enumerate((p0, p1, p2, p3)):
            q[i * part_rows : (i + 1) * part_rows, :] = dot_nn(part[...], weight).astype(BF)
        attend_rows(q, k, v, att, sums, valid)
        finish_sums(sums, lse)

    w_spec = pl.BlockSpec((w_rows, width), lambda *_: (0, column))
    return call(
        kernel,
        (shape((length, width)),) * 2 + (shape((8, length), F32),),
        (1,),
        [SMEM] + [whole((part_rows, model))] * 4 + [w_spec] * 2 + [whole((count, width))] * 2,
        (whole((length, width)),) * 2 + (whole((8, length)),),
        [pltpu.VMEM((pairs, 2, w_rows // pairs, width), BF), pltpu.VMEM((length, lanes), F32)],
        2 * length * model * width + 4 * length * count * width,
        8_000_000,
        (parity, *parts, w_own, w_other, keys, values),
    )


def gate_forward(parity, parts, w_own, w_other):
    part_rows, model = parts[0].shape
    length = part_rows * len(parts)
    hidden = w_own.shape[1] // 2
    block = 512
    steps = hidden // block
    pairs = PAIRS["pairs"]
    w_rows = w_own.shape[0]

    def kernel(par, p0, p1, p2, p3, go, gt, uo, ut, gate, up, act, scr, scr2):
        w_gate = assemble(par[0], go, gt, scr)
        w_up = assemble(par[0], uo, ut, scr2)
        for i, part in enumerate((p0, p1, p2, p3)):
            rows = slice(i * part_rows, (i + 1) * part_rows)
            g = dot_nn(part[...], w_gate)
            u = dot_nn(part[...], w_up)
            gate[rows, :] = g.astype(BF)
            up[rows, :] = u.astype(BF)
            act[rows, :] = (g / (1.0 + jnp.exp2(-LOG2E * g)) * u).astype(BF)

    g_spec = pl.BlockSpec((w_rows, block), lambda j: (0, j))
    u_spec = pl.BlockSpec((w_rows, block), lambda j: (0, steps + j))
    out_spec = pl.BlockSpec((length, block), lambda j: (0, j))
    return call(
        kernel,
        (shape((length, hidden)),) * 3,
        (steps,),
        [SMEM] + [whole((part_rows, model))] * 4 + [g_spec, g_spec, u_spec, u_spec],
        (out_spec,) * 3,
        [pltpu.VMEM((pairs, 2, w_rows // pairs, block), BF)] * 2,
        4 * length * model * hidden,
        22_000_000,
        (parity, *parts, w_own, w_other, w_own, w_other),
    )


def gate_backward(parity, parts, seq, gate, up, d_own, d_other, w_own, w_other):
    part_rows, model = parts[0].shape[1:]
    length = part_rows * len(parts)
    half_rows = length // 2
    hidden = gate.shape[1]
    block = 512
    steps = hidden // block
    pairs = PAIRS["pairs"]
    w_rows = w_own.shape[0]

    def kernel(
        par, p0, p1, p2, p3, g_ref, u_ref, do, dt, go, gt, uo, ut, dgate, dup, keep, send, scr, scr2, scr3, acc
    ):
        j = pl.program_id(0)
        w_down = assemble(par[0], do, dt, scr)
        w_gate = assemble(par[0], go, gt, scr2)
        w_up = assemble(par[0], uo, ut, scr3)

        @pl.when(j == 0)
        def _():
            acc[...] = jnp.zeros_like(acc)

        for i, part in enumerate((p0, p1, p2, p3)):
            rows = slice(i * part_rows, (i + 1) * part_rows)
            d_hidden = dot_nn(part[0], w_down)
            g = g_ref[rows, :].astype(F32)
            u = u_ref[rows, :].astype(F32)
            sig = 1.0 / (1.0 + jnp.exp2(-LOG2E * g))
            d_gate = (d_hidden * u * sig * (1.0 + g * (1.0 - sig))).astype(BF)
            d_up = (d_hidden * (g * sig)).astype(BF)
            dgate[rows, :] = d_gate
            dup[rows, :] = d_up
            acc[rows, :] += dot_nt(d_gate, w_gate) + dot_nt(d_up, w_up)

        @pl.when(j == steps - 1)
        def _():
            keep[...] = acc[:half_rows, :].astype(BF)
            send[...] = acc[half_rows:, :].astype(BF)

    part_spec = pl.BlockSpec((1, part_rows, model), lambda *_: (seq, 0, 0))
    act_spec = pl.BlockSpec((length, block), lambda j: (0, j))
    d_spec = pl.BlockSpec((w_rows, block), lambda j: (0, j))
    u_spec = pl.BlockSpec((w_rows, block), lambda j: (0, steps + j))
    return call(
        kernel,
        (shape((length, hidden)),) * 2 + (shape((half_rows, model)),) * 2,
        (steps,),
        [SMEM] + [part_spec] * 4 + [act_spec] * 2 + [d_spec, d_spec, d_spec, d_spec, u_spec, u_spec],
        (act_spec,) * 2 + (whole((half_rows, model)),) * 2,
        [pltpu.VMEM((pairs, 2, w_rows // pairs, block), BF)] * 3 + [pltpu.VMEM((length, model), F32)],
        6 * length * model * hidden,
        33_000_000,
        (parity, *parts, gate, up, d_own, d_other, w_own, w_other, w_own, w_other),
    )


def cross_backward(parity, parts, w_own, w_other, column_out, column_q, q, keys, values, att, lse, valid):
    part_rows, model = parts[0].shape
    length = part_rows * len(parts)
    half_rows = length // 2
    count, width = keys.shape
    lanes = 2 * HEAD_WIDTH
    pairs = PAIRS["pairs"]
    w_rows = w_own.shape[0]

    def kernel(
        par, p0, p1, p2, p3, oo, ot, qo, qt, q_ref, k_ref, v_ref, a_ref, l_ref, dq, dk, dv, keep, send, scr, do, acc
    ):
        weight = assemble(par[0], oo, ot, scr)
        for i, part in enumerate((p0, p1, p2, p3)):
            do[i * part_rows : (i + 1) * part_rows, :] = dot_nn(part[...], weight).astype(BF)

        def put_k(rows, columns, value):
            dk[rows, columns] = value.astype(BF)

        def put_v(rows, columns, value):
            dv[rows, columns] = value.astype(BF)

        def put_q(columns, value):
            dq[:, columns] = value.astype(BF)

        attend_back(q_ref, k_ref, v_ref, a_ref, do, l_ref, acc, put_k, put_v, put_q, valid)
        weight = assemble(par[0], qo, qt, scr)
        send[...] = dot_nt(dq[half_rows:, :], weight).astype(BF)
        keep[...] = dot_nt(dq[:half_rows, :], weight).astype(BF)

    o_spec = pl.BlockSpec((w_rows, width), lambda *_: (0, column_out))
    q_spec = pl.BlockSpec((w_rows, width), lambda *_: (0, column_q))
    rows_spec = whole((length, width))
    keys_spec = whole((count, width))
    return call(
        kernel,
        (shape((length, width)), shape((count, width)), shape((count, width)))
        + (shape((half_rows, model)),) * 2,
        (1,),
        [SMEM]
        + [whole((part_rows, model))] * 4
        + [o_spec, o_spec, q_spec, q_spec]
        + [rows_spec, keys_spec, keys_spec, rows_spec, whole((8, length))],
        (rows_spec, keys_spec, keys_spec) + (whole((half_rows, model)),) * 2,
        [
            pltpu.VMEM((pairs, 2, w_rows // pairs, width), BF),
            pltpu.VMEM((length, width), BF),
            pltpu.VMEM((length, lanes), F32),
        ],
        4 * length * model * width + 10 * length * count * width,
        12_000_000,
        (parity, *parts, w_own, w_other, w_own, w_other, q, keys, values, att, lse),
    )


def self_backward(parity, parts, o_own, o_other, w_own, w_other, q, k, v, att, lse, cos, low, high):
    part_rows, model = parts[0].shape
    length = part_rows * len(parts)
    half_rows = length // 2
    width = q.shape[1]
    lanes = 2 * HEAD_WIDTH
    pairs = PAIRS["pairs"]
    w_rows = w_own.shape[0]

    def kernel(
        par, p0, p1, p2, p3, oo, ot, wo, wt, q_ref, k_ref, v_ref, a_ref, l_ref, c_ref, lo_ref, h_ref,
        grads, keep, send, scr, scr2, do, acc,
    ):
        weight = assemble(par[0], oo, ot, scr)
        for i, part in enumerate((p0, p1, p2, p3)):
            do[i * part_rows : (i + 1) * part_rows, :] = dot_nn(part[...], weight).astype(BF)

        def put_k(rows, columns, value):
            value = rope(value, c_ref[rows, :], lo_ref[rows, :], h_ref[rows, :], -1.0)
            grads[rows, slice(width + columns.start, width + columns.stop)] = value.astype(BF)

        def put_v(rows, columns, value):
            grads[rows, slice(2 * width + columns.start, 2 * width + columns.stop)] = value.astype(BF)

        def put_q(columns, value):
            grads[:, columns] = rope(value, c_ref[...], lo_ref[...], h_ref[...], -1.0).astype(BF)

        attend_back(q_ref, k_ref, v_ref, a_ref, do, l_ref, acc, put_k, put_v, put_q, length)
        weight = assemble(par[0], wo, wt, scr2)
        send[...] = dot_nt(grads[half_rows:, :], weight).astype(BF)
        keep[...] = dot_nt(grads[:half_rows, :], weight).astype(BF)

    o_spec = pl.BlockSpec((w_rows, width), lambda *_: (0, 0))
    rows_spec = whole((length, width))
    return call(
        kernel,
        (shape((length, 3 * width)),) + (shape((half_rows, model)),) * 2,
        (1,),
        [SMEM]
        + [whole((part_rows, model))] * 4
        + [o_spec] * 2
        + [whole(w_own.shape)] * 2
        + [rows_spec] * 4
        + [whole((8, length))]
        + [whole((length, lanes))] * 3,
        (whole((length, 3 * width)),) + (whole((half_rows, model)),) * 2,
        [
            pltpu.VMEM((pairs, 2, w_rows // pairs, width), BF),
            pltpu.VMEM((pairs, 2, w_rows // pairs, 3 * width), BF),
            pltpu.VMEM((length, width), BF),
            pltpu.VMEM((length, lanes), F32),
        ],
        8 * length * model * width + 10 * length * length * width,
        24_000_000,
        (parity, *parts, o_own, o_other, w_own, w_other, q, k, v, att, lse, cos, low, high),
    )


def weight_grad(parity, lefts, rights, block):
    model = lefts[0].shape[-1]
    total = rights[0].shape[1]
    steps = total // block
    pairs = PAIRS["pairs"]
    count = len(lefts)
    half = model // 2
    per = [left.shape[-2] * (left.shape[0] if left.ndim == 3 else 1) for left in lefts]

    def kernel(par, *refs):
        left_refs = refs[:count]
        right_refs = refs[count : count + len(rights)]
        own, other, acc, scr = refs[count + len(rights) :]
        place = 0
        flat = []
        for right in right_refs:
            flat.append((place, right))
            place += right.shape[0]
        start = 0
        for n, left in enumerate(left_refs):
            rows = left.shape[0]
            base, right = [(b, r) for b, r in flat if b <= start][-1]
            term = dot_tn(left[...], right[start - base : start - base + rows, :])
            if n == 0:
                acc[...] = term
            else:
                acc[...] += term
            start += rows
        split_rows(par[0], acc[...].astype(BF), scr, own, other, slice(None))

    left_specs = [whole(left.shape) for left in lefts]
    right_specs = [pl.BlockSpec((right.shape[0], block), lambda j: (0, j)) for right in rights]
    out_spec = pl.BlockSpec((half, block), lambda j: (0, j))
    return call(
        kernel,
        (shape((half, total)),) * 2,
        (steps,),
        [SMEM] + left_specs + right_specs,
        (out_spec,) * 2,
        [
            pltpu.VMEM((model, block), F32),
            pltpu.VMEM((pairs, 2, model // (2 * pairs), block), BF),
        ],
        2 * sum(per) * model * total,
        sum(per) * (model + total) * 2 + model * total * 2,
        (parity, *lefts, *rights),
    )


def make_body(dp, group):
    pairs = dp // 2
    swap = [(i, i ^ 1) for i in range(dp)]
    lines = [list(range(0, dp, 2)), list(range(1, dp, 2))]
    over_core = [(i, i ^ 1) for i in range(group)]
    over_x = [(i, i ^ 2) for i in range(group)]

    def body(
        tokens,
        context,
        positions,
        seq_mask,
        cotangent,
        norm_gains,
        norm_shifts,
        w_qkv,
        w_self_out,
        w_cross_q,
        w_cross_kv,
        w_cross_out,
        w_gate_up,
        w_down,
    ):
        PAIRS["pairs"] = pairs
        rank = lax.axis_index("dp")
        spot = lax.axis_index("tensor")
        parity = (rank % 2).astype(jnp.int32).reshape(1)
        seqs, part_rows, model = tokens.shape
        length = positions.shape[1]
        ctx_len = context.shape[1]
        rows = w_qkv.shape[1]
        width = w_qkv.shape[2]
        heads = width // HEAD_WIDTH
        hidden = w_down.shape[0]
        ctx_rows = w_cross_kv.shape[1]

        def fetch(local):
            mine = lax.all_gather(local, "dp", axis=0, tiled=True, axis_index_groups=lines)
            return mine, lax.ppermute(mine, "dp", swap)

        def give(own, other):
            got = lax.ppermute(other, "dp", swap)
            return lax.psum_scatter(
                own + got, "dp", scatter_dimension=0, tiled=True, axis_index_groups=lines
            ).astype(F32)

        def core(v):
            return lax.ppermute(v, "tensor", over_core)

        def across(v):
            return lax.ppermute(v, "tensor", over_x)

        def spread(own):
            far = across(own)
            return (own, far, core(own), core(far))

        def gather_sum(keep, send):
            got = core(send)
            part = part_rows
            far = (keep[part:].astype(F32) + got[part:].astype(F32)).astype(BF)
            back = across(far)
            return keep[:part].astype(F32) + got[:part].astype(F32) + back.astype(F32)

        w_one = jnp.transpose(w_qkv, (1, 0, 2)).reshape(rows, 3 * width)
        w_two = jnp.concatenate(
            [w_self_out.T, w_cross_q, w_cross_out.T, w_cross_kv.reshape(rows, width)], axis=1
        )
        w_three = jnp.transpose(w_gate_up, (1, 0, 2)).reshape(rows, 2 * hidden)
        w_four = w_down.T
        qkv_own, qkv_other = fetch(w_one)
        two_own, two_other = fetch(w_two)
        gu_own, gu_other = fetch(w_three)
        dn_own, dn_other = fetch(w_four)

        keep_scale = seq_mask.astype(F32)[:, None, None]
        token_parts = spread(tokens)
        grad_third = cotangent.astype(F32) * keep_scale
        third_parts = spread(grad_third.astype(BF))

        packed = lax.all_gather(
            jnp.concatenate([norm_gains, norm_shifts], axis=0), ("dp", "tensor"), axis=1, tiled=True
        )
        gains = [packed[j : j + 1] for j in range(3)]
        shifts = [packed[3 + j : 4 + j] for j in range(3)]

        order = jnp.stack([spot, spot ^ 2, spot ^ 1, spot ^ 3])
        half_rot = ROT // 2
        lane = jnp.arange(2 * HEAD_WIDTH) % HEAD_WIDTH
        inverse = jnp.exp((lane % half_rot).astype(F32) * (-2.0 * math.log(10000.0) / ROT))
        tables = []
        for s in range(seqs):
            place = jnp.take(positions[s].reshape(group, part_rows), order, axis=0).reshape(length)
            angles = place.astype(F32)[:, None] * inverse[None, :]
            turned = lane < ROT
            sine = jnp.sin(angles)
            tables.append(
                (
                    jnp.where(turned, jnp.cos(angles), 1.0),
                    jnp.where(lane < half_rot, sine, 0.0),
                    jnp.where((lane >= half_rot) & turned, sine, 0.0),
                )
            )

        ctx_pad = -(-ctx_len // 128) * 128
        kv_own = two_own[:, 3 * width :].reshape(pairs, 2, ctx_rows, width)
        kv_other = two_other[:, 3 * width :].reshape(pairs, 2, ctx_rows, width)
        even = parity[0] == 0
        kv_weight = jnp.stack(
            [jnp.where(even, kv_own, kv_other), jnp.where(even, kv_other, kv_own)], axis=1
        )
        kv_weight = jnp.transpose(kv_weight, (2, 0, 1, 3, 4)).reshape(2, pairs * 2 * ctx_rows, width)
        padded = jnp.pad(context, ((0, 0), (0, ctx_pad - ctx_len), (0, 0)))
        cross_kv = jnp.einsum("scd,kdh->skch", padded, kv_weight, preferred_element_type=F32).astype(BF)

        state = [dict() for _ in range(seqs)]
        for s in range(seqs):
            st = state[s]
            st["normed1"], st["q"], st["k"], st["v"], st["att"], st["lse"] = self_forward(
                parity, token_parts, s, gains[0], shifts[0], qkv_own, qkv_other, *tables[s], heads
            )
        for s in range(seqs):
            st = state[s]
            keep, send = project(parity, st["att"], two_own, two_other, 0, model)
            st["first"] = tokens[s].astype(F32) + gather_sum(keep, send)
            st["xhat2"], st["inv2"] = norm_parts(st["first"])
            normed2 = (st["xhat2"] * gains[1] + shifts[1]).astype(BF)
            st["normed2"] = spread(normed2)
        for s in range(seqs):
            st = state[s]
            st["cq"], st["crossed"], st["clse"] = cross_forward(
                parity, st["normed2"], two_own, two_other, 1, cross_kv[s, 0], cross_kv[s, 1], ctx_len
            )
            keep, send = project(parity, st["crossed"], two_own, two_other, 2, model)
            st["second"] = st["first"] + gather_sum(keep, send)
            st["xhat3"], st["inv3"] = norm_parts(st["second"])
            normed3 = (st["xhat3"] * gains[2] + shifts[2]).astype(BF)
            st["normed3"] = spread(normed3)
        for s in range(seqs):
            st = state[s]
            st["gate"], st["up"], st["hidden"] = gate_forward(parity, st["normed3"], gu_own, gu_other)
        outs = []
        for s in range(seqs):
            st = state[s]
            st["dgate"], st["dup"], keep, send = gate_backward(
                parity, third_parts, s, st["gate"], st["up"], dn_own, dn_other, gu_own, gu_other
            )
            st["d_normed3"] = gather_sum(keep, send)
        third_lefts = [part[s] for s in range(seqs) for part in third_parts]
        dn_grad = give(*weight_grad(parity, third_lefts, [st["hidden"] for st in state], 384))
        gate_grad = weight_grad(
            parity, [p for st in state for p in st["normed3"]], [st["dgate"] for st in state], 384
        )
        up_grad = weight_grad(
            parity, [p for st in state for p in st["normed3"]], [st["dup"] for st in state], 384
        )
        gate_part = give(*gate_grad)
        up_part = give(*up_grad)
        for s in range(seqs):
            st = state[s]
            keep, send = project(parity, st["hidden"], dn_own, dn_other, 0, model)
            third = st["second"] + gather_sum(keep, send)
            outs.append((third * keep_scale[s]).astype(BF))

        gain_grads, shift_grads = [0.0] * 3, [0.0] * 3
        for s in range(seqs):
            st = state[s]
            back, gain_term, shift_term = norm_back(st["d_normed3"], st["xhat3"], st["inv3"], gains[2])
            gain_grads[2] += gain_term
            shift_grads[2] += shift_term
            st["d_second"] = grad_third[s] + back
            st["dy2"] = spread(st["d_second"].astype(BF))
        for s in range(seqs):
            st = state[s]
            st["dcq"], st["dck"], st["dcv"], keep, send = cross_backward(
                parity, st["dy2"], two_own, two_other, 2, 1, st["cq"],
                cross_kv[s, 0], cross_kv[s, 1], st["crossed"], st["clse"], ctx_len,
            )
            d_normed2 = gather_sum(keep, send)
            back, gain_term, shift_term = norm_back(d_normed2, st["xhat2"], st["inv2"], gains[1])
            gain_grads[1] += gain_term
            shift_grads[1] += shift_term
            st["d_first"] = st["d_second"] + back
            st["dy1"] = spread(st["d_first"].astype(BF))
        co_grad = weight_grad(
            parity, [p for st in state for p in st["dy2"]], [st["crossed"] for st in state], width
        )
        cq_grad = weight_grad(
            parity, [p for st in state for p in st["normed2"]], [st["dcq"] for st in state], width
        )
        dkv = jnp.stack([jnp.stack([st["dck"], st["dcv"]]) for st in state])[:, :, :ctx_len]
        kv_grad = jnp.einsum("scd,skch->kdh", context, dkv, preferred_element_type=F32).astype(BF)
        kv_grad = jnp.transpose(kv_grad.reshape(2, pairs, 2, ctx_rows, width), (1, 2, 0, 3, 4))
        kv_own_grad = jnp.where(even, kv_grad[:, 0], kv_grad[:, 1]).reshape(pairs * rows, width)
        kv_other_grad = jnp.where(even, kv_grad[:, 1], kv_grad[:, 0]).reshape(pairs * rows, width)
        middle = give(
            jnp.concatenate([co_grad[0], cq_grad[0], kv_own_grad], axis=1),
            jnp.concatenate([co_grad[1], cq_grad[1], kv_other_grad], axis=1),
        )
        for s in range(seqs):
            st = state[s]
            st["dqkv"], keep, send = self_backward(
                parity, st["dy1"], two_own, two_other, qkv_own, qkv_other,
                st["q"], st["k"], st["v"], st["att"], st["lse"], *tables[s],
            )
            st["d_normed1"] = gather_sum(keep, send)
        so_grad = weight_grad(
            parity, [p for st in state for p in st["dy1"]], [st["att"] for st in state], width
        )
        qkv_grad = weight_grad(
            parity, [st["normed1"] for st in state], [st["dqkv"] for st in state], width
        )
        last = give(
            jnp.concatenate([so_grad[0], qkv_grad[0]], axis=1),
            jnp.concatenate([so_grad[1], qkv_grad[1]], axis=1),
        )
        grad_inputs = []
        for s in range(seqs):
            st = state[s]
            xhat, inv = norm_parts(tokens[s].astype(F32))
            back, gain_term, shift_term = norm_back(st["d_normed1"], xhat, inv, gains[0])
            gain_grads[0] += gain_term
            shift_grads[0] += shift_term
            grad_inputs.append(st["d_first"] + back)
        norm_grads = lax.psum_scatter(
            jnp.stack(gain_grads + shift_grads), ("dp", "tensor"), scatter_dimension=1, tiled=True
        )
        return (
            jnp.stack(outs),
            jnp.stack(grad_inputs),
            norm_grads[:3],
            norm_grads[3:],
            jnp.transpose(last[:, width:].reshape(rows, 3, width), (1, 0, 2)),
            last[:, :width].T,
            middle[:, width : 2 * width],
            middle[:, 2 * width :].reshape(2, ctx_rows, width),
            middle[:, :width].T,
            jnp.stack([gate_part, up_part]),
            dn_grad.T,
        )

    return body


def norm_parts(rows):
    mean = jnp.mean(rows, axis=-1, keepdims=True)
    centred = rows - mean
    inv = lax.rsqrt(jnp.mean(centred * centred, axis=-1, keepdims=True) + EPS)
    return centred * inv, inv


def norm_back(grad, xhat, inv, gain):
    scaled = grad * gain
    back = inv * (
        scaled
        - jnp.mean(scaled, axis=-1, keepdims=True)
        - xhat * jnp.mean(scaled * xhat, axis=-1, keepdims=True)
    )
    return back, jnp.sum(grad * xhat, axis=0), jnp.sum(grad, axis=0)


def solution(mesh):
    in_specs = (
        P("dp", "tensor", None),
        P("dp", None, None),
        P("dp", None),
        P("dp"),
        P("dp", "tensor", None),
        P(None, ("dp", "tensor")),
        P(None, ("dp", "tensor")),
        P(None, "dp", "tensor"),
        P("tensor", "dp"),
        P("dp", "tensor"),
        P(None, "dp", "tensor"),
        P("tensor", "dp"),
        P(None, "dp", "tensor"),
        P("tensor", "dp"),
    )
    out_specs = (
        P("dp", "tensor", None),
        P("dp", "tensor", None),
        P(None, ("dp", "tensor")),
        P(None, ("dp", "tensor")),
        P(None, "dp", "tensor"),
        P("tensor", "dp"),
        P("dp", "tensor"),
        P(None, "dp", "tensor"),
        P("tensor", "dp"),
        P(None, "dp", "tensor"),
        P("tensor", "dp"),
    )
    body = make_body(mesh.shape["dp"], mesh.shape["tensor"])
    return jax.shard_map(body, mesh=mesh, in_specs=in_specs, out_specs=out_specs, check_vma=False)
```

```python
import functools
import math

import jax
import jax.numpy as jnp
from jax import lax
from jax.experimental import pallas as pl
from jax.experimental.pallas import tpu as pltpu
from jax.sharding import PartitionSpec as P

HEAD_WIDTH = 64
ROT = 32
EPS = 1e-05
BF = jnp.bfloat16
F32 = jnp.float32
LOG2E = math.log2(math.e)
VMEM_BYTES = 56 * 1024 * 1024


def call(kernel, outs, grid, in_specs, out_specs, scratch, flops, moved, operands):
    return pl.pallas_call(
        kernel,
        out_shape=outs,
        grid=grid,
        in_specs=in_specs,
        out_specs=out_specs,
        scratch_shapes=scratch,
        compiler_params=pltpu.CompilerParams(vmem_limit_bytes=VMEM_BYTES),
        cost_estimate=pl.CostEstimate(flops=flops * 3, bytes_accessed=moved, transcendentals=0),
    )(*operands)


def after(value, *others):
    return lax.optimization_barrier((value, *others))[0]


def shape(dims, kind=BF):
    return jax.ShapeDtypeStruct(dims, kind)


def whole(dims):
    return pl.BlockSpec(dims, lambda *_: (0,) * len(dims))


SMEM = pl.BlockSpec(memory_space=pltpu.SMEM)


def dot_nn(a, b):
    return jnp.dot(a, b, preferred_element_type=F32)


def dot_nt(a, b):
    return lax.dot_general(a, b, (((1,), (1,)), ((), ())), preferred_element_type=F32)


def dot_tn(a, b):
    return lax.dot_general(a, b, (((0,), (0,)), ((), ())), preferred_element_type=F32)


def assemble(parity, own, other, scratch):
    pairs, _, rows, width = scratch.shape
    scratch[:, pl.ds(parity, 1)] = own[...].reshape(pairs, 1, rows, width)
    scratch[:, pl.ds(1 - parity, 1)] = other[...].reshape(pairs, 1, rows, width)
    return scratch[...].reshape(pairs * 2 * rows, width)


def split_rows(parity, value, scratch, own, other, columns):
    pairs, _, rows, width = scratch.shape
    scratch[...] = value.reshape(scratch.shape)
    own[:, columns] = scratch[:, pl.ds(parity, 1)].reshape(pairs * rows, width)
    other[:, columns] = scratch[:, pl.ds(1 - parity, 1)].reshape(pairs * rows, width)


def rope(v, cosine, low_sine, high_sine, sign):
    width = v.shape[-1]
    half = ROT // 2
    ahead = pltpu.roll(v, width - half, 1)
    behind = pltpu.roll(v, half, 1)
    return v * cosine + sign * (behind * high_sine - ahead * low_sine)


def head_mask(h):
    lane = lax.broadcasted_iota(jnp.int32, (1, 2 * HEAD_WIDTH), 1)
    return (lane // HEAD_WIDTH) == h


def attend_rows(q_ref, k_ref, v_ref, att_ref, lse_scratch, valid, base=0):
    length, width = q_ref.shape
    keys = k_ref.shape[0]
    block = min(256, length)
    scale = HEAD_WIDTH**-0.5 * LOG2E
    lanes = 2 * HEAD_WIDTH

    def rows_step(i, _):
        rows = pl.ds(pl.multiple_of(i * block, block), block)
        lane = lax.broadcasted_iota(jnp.int32, (block, lanes), 1)
        sums = lse_scratch[rows, :]
        for pair in range(width // lanes):
            columns = slice(pair * lanes, (pair + 1) * lanes)
            q = q_ref[rows, columns]
            total = None
            for h in range(2):
                mask = head_mask(h)
                k = jnp.where(mask, k_ref[:, columns], jnp.zeros((), BF))
                v = jnp.where(mask, v_ref[:, columns], jnp.zeros((), BF))
                logits = dot_nt(q, k) * scale
                if valid < keys:
                    spot = lax.broadcasted_iota(jnp.int32, logits.shape, 1)
                    logits = jnp.where(spot < valid, logits, -jnp.inf)
                peak = jnp.max(logits, axis=1, keepdims=True)
                weights = jnp.exp2(logits - peak)
                norm = jnp.sum(weights, axis=1, keepdims=True)
                term = dot_nn(weights.astype(BF), v) / norm
                total = term if total is None else total + term
                sums = jnp.where(lane == base + pair * 2 + h, peak + jnp.log2(norm), sums)
            att_ref[rows, columns] = total.astype(BF)
        lse_scratch[rows, :] = sums
        return 0

    lax.fori_loop(0, length // block, rows_step, 0)


def attend_back(q_ref, k_ref, v_ref, att_ref, do_ref, lse_ref, dq_acc, put_k, put_v, put_q, valid, base=0):
    length, width = q_ref.shape
    keys = k_ref.shape[0]
    block = min(256, keys)
    scale = HEAD_WIDTH**-0.5
    lanes = 2 * HEAD_WIDTH
    for pair in range(width // lanes):
        columns = slice(pair * lanes, (pair + 1) * lanes)
        product = do_ref[:, columns].astype(F32) * att_ref[:, columns].astype(F32)
        deltas = []
        for h in range(2):
            ones = jnp.where(head_mask(h), 1.0, 0.0).astype(F32)
            deltas.append(
                lax.dot_general(
                    jnp.broadcast_to(ones, (8, lanes)),
                    product,
                    (((1,), (1,)), ((), ())),
                    preferred_element_type=F32,
                    precision=lax.Precision.HIGHEST,
                )[:1]
            )
        dq_acc[...] = jnp.zeros_like(dq_acc)

        def keys_step(i, _):
            rows = pl.ds(pl.multiple_of(i * block, block), block)
            dk_total, dv_total = None, None
            for h in range(2):
                mask = head_mask(h)
                zero = jnp.zeros((), BF)
                k = jnp.where(mask, k_ref[rows, columns], zero)
                v = jnp.where(mask, v_ref[rows, columns], zero)
                q = q_ref[:, columns]
                do = do_ref[:, columns]
                head = base + pair * 2 + h
                logits = dot_nt(k, q) * (scale * LOG2E)
                weights = jnp.exp2(logits - lse_ref[head : head + 1, :])
                if valid < keys:
                    spot = i * block + lax.broadcasted_iota(jnp.int32, weights.shape, 0)
                    weights = jnp.where(spot < valid, weights, 0.0)
                dp = dot_nt(v, do)
                ds = (weights * (dp - deltas[h])).astype(BF)
                dv = dot_nn(weights.astype(BF), jnp.where(mask, do, zero))
                dk = dot_nn(ds, jnp.where(mask, q, zero))
                dq_acc[...] += dot_tn(ds, k)
                dk_total = dk if dk_total is None else dk_total + dk
                dv_total = dv if dv_total is None else dv_total + dv
            put_k(rows, columns, dk_total * scale)
            put_v(rows, columns, dv_total)
            return 0

        lax.fori_loop(0, keys // block, keys_step, 0)
        put_q(columns, dq_acc[...] * scale)


def finish_sums(lse_scratch, lse_ref):
    lse_ref[...] = jnp.transpose(lse_scratch[...])[: lse_ref.shape[0]]


def row_norm(t):
    mean = jnp.mean(t, axis=-1, keepdims=True)
    centred = t - mean
    return centred * lax.rsqrt(jnp.mean(centred * centred, axis=-1, keepdims=True) + EPS)


def self_forward(parts, seq, gain, shift, w_full, cos, low, high, heads):
    part_rows, model = parts[0].shape[1:]
    length = part_rows * len(parts)
    width = heads * HEAD_WIDTH
    lanes = 2 * HEAD_WIDTH

    def kernel(p0, p1, p2, p3, g, b, weight, c_ref, l_ref, h_ref, normed, q, k, v, att, lse, sums):
        for i, part in enumerate((p0, p1, p2, p3)):
            rows = slice(i * part_rows, (i + 1) * part_rows)
            normed[rows, :] = (row_norm(part[0].astype(F32)) * g[...] + b[...]).astype(BF)
        for j, target in enumerate((q, k, v)):
            value = dot_nn(normed[...], weight[:, j * width : (j + 1) * width])
            if j == 2:
                target[...] = value.astype(BF)
                continue
            for pair in range(width // lanes):
                columns = slice(pair * lanes, (pair + 1) * lanes)
                target[:, columns] = rope(value[:, columns], c_ref[...], l_ref[...], h_ref[...], 1.0).astype(BF)
        sums[...] = jnp.zeros_like(sums)
        attend_rows(q, k, v, att, sums, length)
        finish_sums(sums, lse)

    part_spec = pl.BlockSpec((1, part_rows, model), lambda *_: (seq, 0, 0))
    table_spec = whole((length, lanes))
    return call(
        kernel,
        (shape((length, model)),) + (shape((length, width)),) * 4 + (shape((8, length), F32),),
        (1,),
        [part_spec] * 4 + [whole((1, model))] * 2 + [whole(w_full.shape)] + [table_spec] * 3,
        (whole((length, model)),) + (whole((length, width)),) * 4 + (whole((8, length)),),
        [pltpu.VMEM((length, lanes), F32)],
        2 * length * model * 3 * width + 4 * length * length * width,
        16_000_000,
        (*parts, gain, shift, w_full, cos, low, high),
    )


PAIRS = {}


def project(rows, w_full, column=0):
    length, width = rows.shape
    half_rows = length // 2
    model = w_full.shape[0]

    def kernel(a, weight, keep, send):
        send[...] = dot_nt(a[half_rows:, :], weight[...]).astype(BF)
        keep[...] = dot_nt(a[:half_rows, :], weight[...]).astype(BF)

    return call(
        kernel,
        (shape((half_rows, model)),) * 2,
        (1,),
        [whole((length, width)), pl.BlockSpec((model, width), lambda *_: (0, column))],
        (whole((half_rows, model)),) * 2,
        [],
        2 * length * width * model,
        length * (width + model) * 2 + model * width * 2,
        (rows, w_full),
    )


def norm_terms(t):
    mean = jnp.mean(t, axis=-1, keepdims=True)
    centred = t - mean
    inv = lax.rsqrt(jnp.mean(centred * centred, axis=-1, keepdims=True) + EPS)
    return centred * inv, inv


def add_terms(refs):
    total = refs[0][...].astype(F32)
    for ref in refs[1:]:
        total = total + ref[...].astype(F32)
    return total


def cross_forward(tokens, seq, terms, norms, weights, kv, valid):
    rows, model = terms[2].shape
    parts = len(weights)
    width = weights[0].shape[1] // 2
    count = kv.shape[3]
    lanes = 2 * HEAD_WIDTH
    heads = width // HEAD_WIDTH
    lse_rows = -(-parts * heads // 8) * 8

    def kernel(t, a, b, c, n_ref, w0, w1, w2, w3, kv_ref, first, second, normed2, normed3, q, att, lse, sums):
        value = t[0].astype(F32) + add_terms((a, b, c))
        first[...] = value
        normed2[...] = (norm_terms(value)[0] * n_ref[1:2, :] + n_ref[4:5, :]).astype(BF)
        sums[...] = jnp.zeros_like(sums)
        total = value
        for p, w in enumerate((w0, w1, w2, w3)):
            columns = pl.ds(p * width, width)
            q[:, columns] = dot_nn(normed2[...], w[:, :width]).astype(BF)
            attend_rows(
                q.at[:, columns], kv_ref.at[p, 0, 0], kv_ref.at[p, 0, 1], att.at[:, columns], sums, valid, p * heads
            )
            total = total + dot_nt(att[:, columns], w[:, width:])
        second[...] = total
        normed3[...] = (norm_terms(total)[0] * n_ref[2:3, :] + n_ref[5:6, :]).astype(BF)
        finish_sums(sums, lse)

    rows_spec = whole((rows, model))
    return call(
        kernel,
        (shape((rows, model), F32),) * 2 + (shape((rows, model)),) * 4 + (shape((lse_rows, rows), F32),),
        (1,),
        [pl.BlockSpec((1, rows, model), lambda *_: (seq, 0, 0))]
        + [rows_spec] * 3
        + [whole(norms.shape)]
        + [whole(weights[0].shape)] * 4
        + [pl.BlockSpec((parts, 1, 2, count, width), lambda *_: (0, seq, 0, 0, 0))],
        (rows_spec,) * 6 + (whole((lse_rows, rows)),),
        [pltpu.VMEM((rows, lanes), F32)],
        4 * rows * model * parts * width + 4 * rows * count * parts * width,
        18_000_000,
        (tokens, *terms, norms, *weights, kv),
    )


def norm_pull(grad, t, gain):
    xhat, inv = norm_terms(t)
    scaled = grad * gain
    back = inv * (
        scaled
        - jnp.mean(scaled, axis=-1, keepdims=True)
        - xhat * jnp.mean(scaled * xhat, axis=-1, keepdims=True)
    )
    return back, jnp.sum(grad * xhat, axis=0, keepdims=True), jnp.sum(grad, axis=0, keepdims=True)


def cross_backward(third, seq, terms, second, first, norms, weights, kv, q, att, lse, valid):
    rows, model = terms[2].shape
    parts = len(weights)
    width = weights[0].shape[1] // 2
    count = kv.shape[3]
    lanes = 2 * HEAD_WIDTH
    heads = width // HEAD_WIDTH

    def kernel(
        t, a, b, c, s_ref, f_ref, n_ref, w0, w1, w2, w3, kv_ref, q_ref, a_ref, l_ref,
        d_first, dy2, dy1, dq, dkv, stats, do, acc,
    ):
        back, gain3, shift3 = norm_pull(add_terms((a, b, c)), s_ref[...], n_ref[2:3, :])
        d_second = t[0].astype(F32) + back
        dy2[...] = d_second.astype(BF)
        d_normed2 = None
        for p, w in enumerate((w0, w1, w2, w3)):
            columns = pl.ds(p * width, width)
            do[...] = dot_nn(dy2[...], w[:, width:]).astype(BF)

            def put_k(rows_at, at, value, p=p):
                dkv[p, 0, rows_at, at] = value.astype(BF)

            def put_v(rows_at, at, value, p=p):
                dkv[p, 1, rows_at, at] = value.astype(BF)

            def put_q(at, value, p=p):
                dq[:, slice(p * width + at.start, p * width + at.stop)] = value.astype(BF)

            attend_back(
                q_ref.at[:, columns], kv_ref.at[p, 0, 0], kv_ref.at[p, 0, 1], a_ref.at[:, columns], do, l_ref, acc,
                put_k, put_v, put_q, valid, p * heads,
            )
            term = dot_nt(dq[:, columns], w[:, :width])
            d_normed2 = term if d_normed2 is None else d_normed2 + term
        back, gain2, shift2 = norm_pull(d_normed2, f_ref[...], n_ref[1:2, :])
        value = d_second + back
        d_first[...] = value
        dy1[...] = value.astype(BF)
        stats[...] = jnp.concatenate([gain2, gain3, shift2, shift3, jnp.zeros((4, model), F32)], axis=0)

    rows_spec = whole((rows, model))
    return call(
        kernel,
        (shape((rows, model), F32),)
        + (shape((rows, model)),) * 3
        + (shape((parts, 2, count, width)), shape((8, model), F32)),
        (1,),
        [pl.BlockSpec((1, rows, model), lambda *_: (seq, 0, 0))]
        + [rows_spec] * 5
        + [whole(norms.shape)]
        + [whole(weights[0].shape)] * 4
        + [pl.BlockSpec((parts, 1, 2, count, width), lambda *_: (0, seq, 0, 0, 0))]
        + [rows_spec] * 2
        + [whole(lse.shape)],
        (rows_spec,) * 4 + (whole((parts, 2, count, width)), whole((8, model))),
        [pltpu.VMEM((rows, width), BF), pltpu.VMEM((rows, lanes), F32)],
        4 * rows * model * parts * width + 10 * rows * count * parts * width,
        24_000_000,
        (third, *terms, second, first, norms, *weights, kv, q, att, lse),
    )


def cross_weight_grad(parity, normed, dys, dqs, atts, parts):
    seqs = len(dys)
    rows, model = dys[0].shape
    width = model // parts
    pairs = PAIRS["pairs"]
    half = model // 2

    def kernel(par, *refs):
        n_refs, y_refs, q_refs, a_refs = (refs[i * seqs : (i + 1) * seqs] for i in range(4))
        outs = refs[4 * seqs : 4 * seqs + parts]
        scr = refs[-1]
        for p in range(parts):
            at = slice(p * width, (p + 1) * width)
            for j, (lefts, rights) in enumerate(((n_refs, q_refs), (y_refs, a_refs))):
                value = None
                for left, right in zip(lefts, rights):
                    term = dot_tn(left[...], right[:, at])
                    value = term if value is None else value + term
                scr[...] = value.astype(BF).reshape(scr.shape)
                columns = slice(j * width, (j + 1) * width)
                outs[p][0, :, columns] = scr[:, pl.ds(par[0], 1)].reshape(half, width)
                outs[p][1, :, columns] = scr[:, pl.ds(1 - par[0], 1)].reshape(half, width)

    return call(
        kernel,
        (shape((2, half, 2 * width)),) * parts,
        (1,),
        [SMEM] + [whole((rows, model))] * (4 * seqs),
        (whole((2, half, 2 * width)),) * parts,
        [pltpu.VMEM((pairs, 2, half // pairs, width), BF)],
        4 * seqs * rows * model * model,
        16_000_000,
        (parity, *normed, *dys, *dqs, *atts),
    )


def gate_forward(parts, weights):
    part_rows, model = parts[0].shape
    length = part_rows * len(parts)
    hidden = weights.shape[2]
    block = 512
    steps = hidden // block

    def kernel(p0, p1, p2, p3, wg, wu, gate, up, act):
        for i, part in enumerate((p0, p1, p2, p3)):
            rows = slice(i * part_rows, (i + 1) * part_rows)
            g = dot_nn(part[...], wg[0])
            u = dot_nn(part[...], wu[0])
            gate[rows, :] = g.astype(BF)
            up[rows, :] = u.astype(BF)
            act[rows, :] = (g / (1.0 + jnp.exp2(-LOG2E * g)) * u).astype(BF)

    g_spec = pl.BlockSpec((1, model, block), lambda j: (0, 0, j))
    u_spec = pl.BlockSpec((1, model, block), lambda j: (1, 0, j))
    out_spec = pl.BlockSpec((length, block), lambda j: (0, j))
    return call(
        kernel,
        (shape((length, hidden)),) * 3,
        (steps,),
        [whole((part_rows, model))] * 4 + [g_spec, u_spec],
        (out_spec,) * 3,
        [],
        4 * length * model * hidden,
        22_000_000,
        (*parts, weights, weights),
    )


def gate_backward(parts, seq, gate, up, w_down, weights):
    part_rows, model = parts[0].shape[1:]
    length = part_rows * len(parts)
    half_rows = length // 2
    hidden = gate.shape[1]
    block = 512
    steps = hidden // block

    def kernel(p0, p1, p2, p3, g_ref, u_ref, wd, wg, wu, dgate, dup, keep, send, acc):
        j = pl.program_id(0)

        @pl.when(j == 0)
        def _():
            acc[...] = jnp.zeros_like(acc)

        for i, part in enumerate((p0, p1, p2, p3)):
            rows = slice(i * part_rows, (i + 1) * part_rows)
            d_hidden = dot_nn(part[0], wd[...])
            g = g_ref[rows, :].astype(F32)
            u = u_ref[rows, :].astype(F32)
            sig = 1.0 / (1.0 + jnp.exp2(-LOG2E * g))
            d_gate = (d_hidden * u * sig * (1.0 + g * (1.0 - sig))).astype(BF)
            d_up = (d_hidden * (g * sig)).astype(BF)
            dgate[rows, :] = d_gate
            dup[rows, :] = d_up
            acc[rows, :] += dot_nt(d_gate, wg[0]) + dot_nt(d_up, wu[0])

        @pl.when(j == steps - 1)
        def _():
            keep[...] = acc[:half_rows, :].astype(BF)
            send[...] = acc[half_rows:, :].astype(BF)

    part_spec = pl.BlockSpec((1, part_rows, model), lambda *_: (seq, 0, 0))
    act_spec = pl.BlockSpec((length, block), lambda j: (0, j))
    w_spec = pl.BlockSpec((model, block), lambda j: (0, j))
    g_spec = pl.BlockSpec((1, model, block), lambda j: (0, 0, j))
    u_spec = pl.BlockSpec((1, model, block), lambda j: (1, 0, j))
    return call(
        kernel,
        (shape((length, hidden)),) * 2 + (shape((half_rows, model)),) * 2,
        (steps,),
        [part_spec] * 4 + [act_spec] * 2 + [w_spec, g_spec, u_spec],
        (act_spec,) * 2 + (whole((half_rows, model)),) * 2,
        [pltpu.VMEM((length, model), F32)],
        6 * length * model * hidden,
        33_000_000,
        (*parts, gate, up, w_down, weights, weights),
    )


def self_backward(parts, o_full, w_full, q, k, v, att, lse, cos, low, high):
    part_rows, model = parts[0].shape
    length = part_rows * len(parts)
    half_rows = length // 2
    width = q.shape[1]
    lanes = 2 * HEAD_WIDTH

    def kernel(
        p0, p1, p2, p3, o_ref, w_ref, q_ref, k_ref, v_ref, a_ref, l_ref, c_ref, lo_ref, h_ref,
        grads, keep, send, do, acc,
    ):
        for i, part in enumerate((p0, p1, p2, p3)):
            do[i * part_rows : (i + 1) * part_rows, :] = dot_nn(part[...], o_ref[...]).astype(BF)

        def put_k(rows, columns, value):
            value = rope(value, c_ref[rows, :], lo_ref[rows, :], h_ref[rows, :], -1.0)
            grads[rows, slice(width + columns.start, width + columns.stop)] = value.astype(BF)

        def put_v(rows, columns, value):
            grads[rows, slice(2 * width + columns.start, 2 * width + columns.stop)] = value.astype(BF)

        def put_q(columns, value):
            grads[:, columns] = rope(value, c_ref[...], lo_ref[...], h_ref[...], -1.0).astype(BF)

        attend_back(q_ref, k_ref, v_ref, a_ref, do, l_ref, acc, put_k, put_v, put_q, length)
        send[...] = dot_nt(grads[half_rows:, :], w_ref[...]).astype(BF)
        keep[...] = dot_nt(grads[:half_rows, :], w_ref[...]).astype(BF)

    o_spec = pl.BlockSpec((model, width), lambda *_: (0, 2))
    rows_spec = whole((length, width))
    return call(
        kernel,
        (shape((length, 3 * width)),) + (shape((half_rows, model)),) * 2,
        (1,),
        [whole((part_rows, model))] * 4
        + [o_spec]
        + [whole(w_full.shape)]
        + [rows_spec] * 4
        + [whole((8, length))]
        + [whole((length, lanes))] * 3,
        (whole((length, 3 * width)),) + (whole((half_rows, model)),) * 2,
        [
            pltpu.VMEM((length, width), BF),
            pltpu.VMEM((length, lanes), F32),
        ],
        8 * length * model * width + 10 * length * length * width,
        24_000_000,
        (*parts, o_full, w_full, q, k, v, att, lse, cos, low, high),
    )


def weight_grad(parity, lefts, rights, block, first=0, steps=None):
    model = lefts[0].shape[-1]
    steps = steps or rights[0].shape[1] // block
    total = steps * block
    pairs = PAIRS["pairs"]
    count = len(lefts)
    half = model // 2
    length = sum(left.shape[0] for left in lefts)

    def kernel(par, *refs):
        left_refs = refs[:count]
        right_refs = refs[count : count + len(rights)]
        own, other, rows_scr, scr = refs[count + len(rights) :]

        @pl.when(pl.program_id(0) == 0)
        def _():
            start = 0
            for left in left_refs:
                rows_scr[start : start + left.shape[0], :] = left[...]
                start += left.shape[0]

        start = 0
        value = None
        for right in right_refs:
            term = dot_tn(rows_scr[start : start + right.shape[0], :], right[...])
            value = term if value is None else value + term
            start += right.shape[0]
        split_rows(par[0], value.astype(BF), scr, own, other, slice(None))

    left_specs = [whole(left.shape) for left in lefts]
    right_specs = [pl.BlockSpec((right.shape[0], block), lambda j: (0, first + j)) for right in rights]
    return call(
        kernel,
        (shape((half, total)),) * 2,
        (steps,),
        [SMEM] + left_specs + right_specs,
        (pl.BlockSpec((half, block), lambda j: (0, j)),) * 2,
        [pltpu.VMEM((length, model), BF), pltpu.VMEM((pairs, 2, model // (2 * pairs), block), BF)],
        2 * length * model * total,
        length * (model + total) * 2 + model * total * 2,
        (parity, *lefts, *rights),
    )


def make_body(dp, group):
    pairs = dp // 2
    swap = [(i, i ^ 1) for i in range(dp)]
    lines = [list(range(0, dp, 2)), list(range(1, dp, 2))]
    over_core = [(i, i ^ 1) for i in range(group)]
    over_x = [(i, i ^ 2) for i in range(group)]

    def body(
        tokens,
        context,
        positions,
        seq_mask,
        cotangent,
        norm_gains,
        norm_shifts,
        w_qkv,
        w_self_out,
        w_cross_q,
        w_cross_kv,
        w_cross_out,
        w_gate_up,
        w_down,
    ):
        PAIRS["pairs"] = pairs
        rank = lax.axis_index("dp")
        spot = lax.axis_index("tensor")
        parity = (rank % 2).astype(jnp.int32).reshape(1)
        seqs, part_rows, model = tokens.shape
        length = positions.shape[1]
        ctx_len = context.shape[1]
        rows = w_qkv.shape[1]
        width = w_qkv.shape[2]
        heads = width // HEAD_WIDTH
        hidden = w_down.shape[0]
        ctx_rows = w_cross_kv.shape[1]

        turns = {}

        def in_turn(axis, v, pairs_of, name):
            if axis in turns:
                v = after(v, turns[axis])
            turns[axis] = lax.ppermute(v, name, pairs_of)
            return turns[axis]

        def fetch_all(local):
            return lax.all_gather(local, "dp", axis=0, tiled=True)

        def pair_sum(own, other, *ready):
            got = in_turn("y", other, swap, "dp")
            return own + after(got, *ready)

        def line_sum(v):
            return lax.psum_scatter(v, "dp", scatter_dimension=0, tiled=True, axis_index_groups=lines).astype(F32)

        def core(v):
            return lax.ppermute(v, "tensor", over_core)

        def across(v):
            return in_turn("x", v, over_x, "tensor")

        def spread(own):
            far = across(own)
            return (own, far, core(own), core(far))

        def reduce_rows(keep, send):
            got = core(send)
            far = (keep[part_rows:].astype(F32) + got[part_rows:].astype(F32)).astype(BF)
            return keep, got, across(far)

        def gather_sum(keep, got, back):
            return keep[:part_rows].astype(F32) + got[:part_rows].astype(F32) + back.astype(F32)

        def reduce_parts(own, far, near, both):
            own = (own.astype(F32) + core(near).astype(F32)).astype(BF)
            far = (far.astype(F32) + core(both).astype(F32)).astype(BF)
            return own, across(far)

        def total_of(v):
            for bit in range((group - 1).bit_length()):
                v = v + lax.ppermute(v, "tensor", [(i, i ^ (1 << bit)) for i in range(group)])
            for bit in range((dp - 1).bit_length()):
                v = v + lax.ppermute(v, "dp", [(i, i ^ (1 << bit)) for i in range(dp)])
            return v

        place = rank * group + spot
        mine = jnp.concatenate([norm_gains, norm_shifts], axis=0)
        share = mine.shape[1]
        norms = total_of(lax.dynamic_update_slice(jnp.zeros((6, model), F32), mine, (0, place * share)))
        gains = [norms[j : j + 1] for j in range(3)]
        shifts = [norms[3 + j : 4 + j] for j in range(3)]
        keep_scale = seq_mask.astype(F32)[:, None, None]
        grad_third = cotangent.astype(F32) * keep_scale
        token_parts = spread(after(tokens, norms))
        third_parts = spread(after(grad_third.astype(BF), token_parts[1]))

        w_one = jnp.transpose(w_qkv, (1, 0, 2)).reshape(rows, 3 * width)
        qkv_full = fetch_all(w_one)
        w_two = jnp.concatenate(
            [w_cross_q, w_cross_out.T, w_self_out.T, w_cross_kv.reshape(rows, width)], axis=1
        )
        two_full = fetch_all(after(w_two, qkv_full, token_parts[1]))

        order = jnp.stack([spot, spot ^ 2, spot ^ 1, spot ^ 3])
        half_rot = ROT // 2
        lane = jnp.arange(2 * HEAD_WIDTH) % HEAD_WIDTH
        inverse = jnp.exp((lane % half_rot).astype(F32) * (-2.0 * math.log(10000.0) / ROT))
        tables = []
        for s in range(seqs):
            spots = jnp.take(positions[s].reshape(group, part_rows), order, axis=0).reshape(length)
            angles = spots.astype(F32)[:, None] * inverse[None, :]
            turned = lane < ROT
            sine = jnp.sin(angles)
            tables.append(
                (
                    jnp.where(turned, jnp.cos(angles), 1.0),
                    jnp.where(lane < half_rot, sine, 0.0),
                    jnp.where((lane >= half_rot) & turned, sine, 0.0),
                )
            )

        state = [dict() for _ in range(seqs)]
        for s in range(seqs):
            st = state[s]
            gain = gains[0]
            if s > 0:
                gain = after(gain, state[0]["att"], third_parts[1])
            st["normed1"], st["q"], st["k"], st["v"], st["att"], st["lse"] = self_forward(
                token_parts, s, gain, shifts[0], qkv_full, *tables[s], heads
            )
        last = state[seqs - 1]["att"]
        two_full = after(two_full, last)
        gu_full = lax.all_gather(after(w_gate_up, two_full), "dp", axis=1, tiled=True)
        cross_full = two_full[:, : 2 * width]

        ctx_pad = -(-ctx_len // 128) * 128
        kv_weight = jnp.transpose(two_full[:, 3 * width :].reshape(dp, 2, ctx_rows, width), (1, 0, 2, 3))
        kv_weight = kv_weight.reshape(2, dp * ctx_rows, width)
        cross_kv = jnp.einsum("scd,kdh->skch", context, kv_weight, preferred_element_type=F32).astype(BF)
        cross_kv = jnp.stack(spread(cross_kv))
        cross_kv = jnp.pad(cross_kv, ((0, 0), (0, 0), (0, 0), (0, ctx_pad - ctx_len), (0, 0)))

        for s in range(seqs):
            st = state[s]
            st["terms"] = reduce_rows(*project(after(st["att"], last), two_full, 2))
            last = st["terms"][0]
        cross_parts = spread(cross_full)
        for s in range(seqs):
            st = state[s]
            terms = st["terms"]
            if s > 0:
                terms = (after(terms[0], gu_full), *terms[1:])
            st["first"], st["second"], st["normed2"], normed3, st["cq"], st["crossed"], st["clse"] = cross_forward(
                tokens, s, terms, norms, cross_parts, cross_kv, ctx_len
            )
            st["normed3"] = spread(normed3)
        dn_full = fetch_all(after(w_down.T, gu_full))
        for s in range(seqs):
            st = state[s]
            st["gate"], st["up"], st["hidden"] = gate_forward(st["normed3"], gu_full)
        third_lefts = [part[s] for s in range(seqs) for part in third_parts]
        dn_pair = weight_grad(parity, third_lefts, [st["hidden"] for st in state], 384)
        last = dn_pair[1]
        for s in range(seqs):
            st = state[s]
            st["dgate"], st["dup"], keep, send = gate_backward(
                third_parts, s, after(st["gate"], last), st["up"], dn_full, gu_full
            )
            last = keep
            st["d_normed3"] = reduce_rows(keep, send)
        dn_sum = pair_sum(*dn_pair, last)
        dn_grad = line_sum(dn_sum)
        normed3 = [p for st in state for p in st["normed3"]]
        gate_pair = weight_grad(parity, normed3, [after(st["dgate"], dn_sum) for st in state], 384)
        up_pair = weight_grad(parity, normed3, [after(st["dup"], gate_pair[1]) for st in state], 384)

        gain_grads, shift_grads = [0.0] * 3, [0.0] * 3
        last = up_pair[1]
        for s in range(seqs):
            st = state[s]
            st["d_first"], st["dy2"], dy1, st["dcq"], st["dkv"], stats = cross_backward(
                third_parts[0], s, st["d_normed3"], st["second"], after(st["first"], last), norms, cross_parts,
                cross_kv, st["cq"], st["crossed"], st["clse"], ctx_len,
            )
            last = dy1
            for j in range(1, 3):
                gain_grads[j] += stats[j - 1]
                shift_grads[j] += stats[j + 1]
            st["dy1"] = spread(dy1)
        gate_sum = pair_sum(*gate_pair, last)
        gate_part = line_sum(after(gate_sum, dn_grad))
        cross_terms = cross_weight_grad(
            parity,
            [after(st["normed2"], last, state[0]["dy1"][1]) for st in state],
            [st["dy2"] for st in state],
            [st["dcq"] for st in state],
            [st["crossed"] for st in state],
            group,
        )
        last = cross_terms[0]
        for s in range(seqs):
            st = state[s]
            st["out_terms"] = project(after(st["hidden"], last), dn_full)
            last = st["out_terms"][0]
        dkv_own, dkv_far = reduce_parts(*(jnp.stack([st["dkv"][p] for st in state]) for p in range(group)))
        cross_mine, cross_far = reduce_parts(*cross_terms)
        last = (last, dn_grad, gate_sum, *(p for st in state for p in st["dy1"]))
        for s in range(seqs):
            st = state[s]
            st["dqkv"], keep, send = self_backward(
                st["dy1"], two_full, qkv_full,
                after(st["q"], *last), st["k"], st["v"], st["att"], st["lse"], *tables[s],
            )
            last = keep
            st["d_normed1"] = (keep, send)
            if s > 0:
                continue
            up_sum = pair_sum(*up_pair, last)
            up_part = line_sum(after(up_sum, gate_part))
            so_pair = weight_grad(
                parity,
                [p for st in state for p in st["dy1"]],
                [after(st["att"], last, gate_part) for st in state],
                width,
            )
            dkv = (dkv_own.astype(F32) + after(dkv_far, last).astype(F32)).astype(BF)[:, :, :ctx_len]
            kv_grad = jnp.einsum("scd,skch->kdh", context, dkv, preferred_element_type=F32).astype(BF)
            kv_grad = jnp.transpose(kv_grad.reshape(2, pairs, 2, ctx_rows, width), (1, 2, 0, 3, 4))
            even = parity[0] == 0
            kv_mine = jnp.where(even, kv_grad[:, 0], kv_grad[:, 1]).reshape(pairs * rows, width)
            kv_other = jnp.where(even, kv_grad[:, 1], kv_grad[:, 0]).reshape(pairs * rows, width)
            cross_sum = cross_mine + after(cross_far, so_pair)
            middle_pair = [
                jnp.concatenate(v, axis=1)
                for v in ((cross_sum[0], kv_mine, so_pair[0]), (cross_sum[1], kv_other, so_pair[1]))
            ]
            last = (up_sum, *middle_pair)
        middle_sum = pair_sum(*middle_pair, keep)
        normed1 = [st["normed1"] for st in state]
        qkv_pairs = []
        for first, steps in ((0, 1), (1, 2)):
            ready = qkv_pairs[0][1] if first else up_part
            dqkv = [after(st["dqkv"], ready) for st in state]
            qkv_pairs.append(weight_grad(parity, normed1, dqkv, width, first, steps))
        middle = line_sum(after(middle_sum, up_part))
        for st in state:
            st["out_terms"] = reduce_rows(*st["out_terms"])
        for st in state:
            st["d_normed1"] = reduce_rows(*st["d_normed1"])
        q_part = line_sum(after(pair_sum(*qkv_pairs[0], qkv_pairs[1][0]), middle))
        kv_part = line_sum(after(pair_sum(*qkv_pairs[1], *(st["d_normed1"][2] for st in state)), q_part))
        qkv_part = jnp.concatenate([q_part, kv_part], axis=1)
        outs = []
        for s in range(seqs):
            st = state[s]
            third = st["second"] + gather_sum(*st["out_terms"])
            outs.append((third * keep_scale[s]).astype(BF))
        grad_inputs = []
        for s in range(seqs):
            st = state[s]
            xhat, inv = norm_parts(tokens[s].astype(F32))
            back, gain_term, shift_term = norm_back(
                gather_sum(*(after(v, qkv_pairs[1][1]) for v in st["d_normed1"])), xhat, inv, gains[0]
            )
            gain_grads[0] += gain_term
            shift_grads[0] += shift_term
            grad_inputs.append(st["d_first"] + back)
        norm_grads = lax.dynamic_slice(
            total_of(jnp.stack(gain_grads + shift_grads)), (0, place * share), (6, share)
        )
        return (
            jnp.stack(outs),
            jnp.stack(grad_inputs),
            norm_grads[:3],
            norm_grads[3:],
            jnp.transpose(qkv_part.reshape(rows, 3, width), (1, 0, 2)),
            middle[:, 3 * width :].T,
            middle[:, :width],
            middle[:, 2 * width : 3 * width].reshape(2, ctx_rows, width),
            middle[:, width : 2 * width].T,
            jnp.stack([gate_part, up_part]),
            dn_grad.T,
        )

    return body


def norm_parts(rows):
    mean = jnp.mean(rows, axis=-1, keepdims=True)
    centred = rows - mean
    inv = lax.rsqrt(jnp.mean(centred * centred, axis=-1, keepdims=True) + EPS)
    return centred * inv, inv


def norm_back(grad, xhat, inv, gain):
    scaled = grad * gain
    back = inv * (
        scaled
        - jnp.mean(scaled, axis=-1, keepdims=True)
        - xhat * jnp.mean(scaled * xhat, axis=-1, keepdims=True)
    )
    return back, jnp.sum(grad * xhat, axis=0), jnp.sum(grad, axis=0)


def solution(mesh):
    in_specs = (
        P("dp", "tensor", None),
        P("dp", None, None),
        P("dp", None),
        P("dp"),
        P("dp", "tensor", None),
        P(None, ("dp", "tensor")),
        P(None, ("dp", "tensor")),
        P(None, "dp", "tensor"),
        P("tensor", "dp"),
        P("dp", "tensor"),
        P(None, "dp", "tensor"),
        P("tensor", "dp"),
        P(None, "dp", "tensor"),
        P("tensor", "dp"),
    )
    out_specs = (
        P("dp", "tensor", None),
        P("dp", "tensor", None),
        P(None, ("dp", "tensor")),
        P(None, ("dp", "tensor")),
        P(None, "dp", "tensor"),
        P("tensor", "dp"),
        P("dp", "tensor"),
        P(None, "dp", "tensor"),
        P("tensor", "dp"),
        P(None, "dp", "tensor"),
        P("tensor", "dp"),
    )
    body = make_body(mesh.shape["dp"], mesh.shape["tensor"])
    return jax.shard_map(body, mesh=mesh, in_specs=in_specs, out_specs=out_specs, check_vma=False)
```

```python
import functools
import math

import jax
import jax.numpy as jnp
from jax import lax
from jax.experimental import pallas as pl
from jax.experimental.pallas import tpu as pltpu
from jax.sharding import PartitionSpec as P

HEAD_WIDTH = 64
ROT = 32
EPS = 1e-05
BF = jnp.bfloat16
F32 = jnp.float32
LOG2E = math.log2(math.e)
VMEM_BYTES = 56 * 1024 * 1024


def call(kernel, outs, grid, in_specs, out_specs, scratch, flops, moved, operands):
    return pl.pallas_call(
        kernel,
        out_shape=outs,
        grid=grid,
        in_specs=in_specs,
        out_specs=out_specs,
        scratch_shapes=scratch,
        compiler_params=pltpu.CompilerParams(vmem_limit_bytes=VMEM_BYTES),
        cost_estimate=pl.CostEstimate(flops=flops * 3, bytes_accessed=moved, transcendentals=0),
    )(*operands)


def after(value, *others):
    return lax.optimization_barrier((value, *others))[0]


def shape(dims, kind=BF):
    return jax.ShapeDtypeStruct(dims, kind)


def whole(dims):
    return pl.BlockSpec(dims, lambda *_: (0,) * len(dims))


SMEM = pl.BlockSpec(memory_space=pltpu.SMEM)


def dot_nn(a, b):
    return jnp.dot(a, b, preferred_element_type=F32)


def dot_nt(a, b):
    return lax.dot_general(a, b, (((1,), (1,)), ((), ())), preferred_element_type=F32)


def dot_tn(a, b):
    return lax.dot_general(a, b, (((0,), (0,)), ((), ())), preferred_element_type=F32)


def assemble(parity, own, other, scratch):
    pairs, _, rows, width = scratch.shape
    scratch[:, pl.ds(parity, 1)] = own[...].reshape(pairs, 1, rows, width)
    scratch[:, pl.ds(1 - parity, 1)] = other[...].reshape(pairs, 1, rows, width)
    return scratch[...].reshape(pairs * 2 * rows, width)


def split_rows(parity, value, scratch, own, other, columns):
    pairs, _, rows, width = scratch.shape
    scratch[...] = value.reshape(scratch.shape)
    own[:, columns] = scratch[:, pl.ds(parity, 1)].reshape(pairs * rows, width)
    other[:, columns] = scratch[:, pl.ds(1 - parity, 1)].reshape(pairs * rows, width)


def rope(v, cosine, low_sine, high_sine, sign):
    width = v.shape[-1]
    half = ROT // 2
    ahead = pltpu.roll(v, width - half, 1)
    behind = pltpu.roll(v, half, 1)
    return v * cosine + sign * (behind * high_sine - ahead * low_sine)


def head_mask(h):
    lane = lax.broadcasted_iota(jnp.int32, (1, 2 * HEAD_WIDTH), 1)
    return (lane // HEAD_WIDTH) == h


def attend_rows(q_ref, k_ref, v_ref, att_ref, lse_scratch, valid, base=0):
    length, width = q_ref.shape
    keys = k_ref.shape[0]
    block = min(256, length)
    scale = HEAD_WIDTH**-0.5 * LOG2E
    lanes = 2 * HEAD_WIDTH

    def rows_step(i, _):
        rows = pl.ds(pl.multiple_of(i * block, block), block)
        lane = lax.broadcasted_iota(jnp.int32, (block, lanes), 1)
        sums = lse_scratch[rows, :]
        for pair in range(width // lanes):
            columns = slice(pair * lanes, (pair + 1) * lanes)
            q = q_ref[rows, columns]
            total = None
            for h in range(2):
                mask = head_mask(h)
                k = jnp.where(mask, k_ref[:, columns], jnp.zeros((), BF))
                v = jnp.where(mask, v_ref[:, columns], jnp.zeros((), BF))
                logits = dot_nt(q, k) * scale
                if valid < keys:
                    spot = lax.broadcasted_iota(jnp.int32, logits.shape, 1)
                    logits = jnp.where(spot < valid, logits, -jnp.inf)
                peak = jnp.max(logits, axis=1, keepdims=True)
                weights = jnp.exp2(logits - peak)
                norm = jnp.sum(weights, axis=1, keepdims=True)
                term = dot_nn(weights.astype(BF), v) / norm
                total = term if total is None else total + term
                sums = jnp.where(lane == base + pair * 2 + h, peak + jnp.log2(norm), sums)
            att_ref[rows, columns] = total.astype(BF)
        lse_scratch[rows, :] = sums
        return 0

    lax.fori_loop(0, length // block, rows_step, 0)


def attend_back(q_ref, k_ref, v_ref, att_ref, do_ref, lse_ref, dq_acc, put_k, put_v, put_q, valid, base=0):
    length, width = q_ref.shape
    keys = k_ref.shape[0]
    block = min(256, keys)
    scale = HEAD_WIDTH**-0.5
    lanes = 2 * HEAD_WIDTH
    for pair in range(width // lanes):
        columns = slice(pair * lanes, (pair + 1) * lanes)
        product = do_ref[:, columns].astype(F32) * att_ref[:, columns].astype(F32)
        deltas = []
        for h in range(2):
            ones = jnp.where(head_mask(h), 1.0, 0.0).astype(F32)
            deltas.append(
                lax.dot_general(
                    jnp.broadcast_to(ones, (8, lanes)),
                    product,
                    (((1,), (1,)), ((), ())),
                    preferred_element_type=F32,
                    precision=lax.Precision.HIGHEST,
                )[:1]
            )
        dq_acc[...] = jnp.zeros_like(dq_acc)

        def keys_step(i, _):
            rows = pl.ds(pl.multiple_of(i * block, block), block)
            dk_total, dv_total = None, None
            for h in range(2):
                mask = head_mask(h)
                zero = jnp.zeros((), BF)
                k = jnp.where(mask, k_ref[rows, columns], zero)
                v = jnp.where(mask, v_ref[rows, columns], zero)
                q = q_ref[:, columns]
                do = do_ref[:, columns]
                head = base + pair * 2 + h
                logits = dot_nt(k, q) * (scale * LOG2E)
                weights = jnp.exp2(logits - lse_ref[head : head + 1, :])
                if valid < keys:
                    spot = i * block + lax.broadcasted_iota(jnp.int32, weights.shape, 0)
                    weights = jnp.where(spot < valid, weights, 0.0)
                dp = dot_nt(v, do)
                ds = (weights * (dp - deltas[h])).astype(BF)
                dv = dot_nn(weights.astype(BF), jnp.where(mask, do, zero))
                dk = dot_nn(ds, jnp.where(mask, q, zero))
                dq_acc[...] += dot_tn(ds, k)
                dk_total = dk if dk_total is None else dk_total + dk
                dv_total = dv if dv_total is None else dv_total + dv
            put_k(rows, columns, dk_total * scale)
            put_v(rows, columns, dv_total)
            return 0

        lax.fori_loop(0, keys // block, keys_step, 0)
        put_q(columns, dq_acc[...] * scale)


def finish_sums(lse_scratch, lse_ref):
    lse_ref[...] = jnp.transpose(lse_scratch[...])[: lse_ref.shape[0]]


def row_norm(t):
    mean = jnp.mean(t, axis=-1, keepdims=True)
    centred = t - mean
    return centred * lax.rsqrt(jnp.mean(centred * centred, axis=-1, keepdims=True) + EPS)


def self_forward(parts, seq, gain, shift, w_full, cos, low, high, heads):
    part_rows, model = parts[0].shape[1:]
    length = part_rows * len(parts)
    width = heads * HEAD_WIDTH
    lanes = 2 * HEAD_WIDTH

    def kernel(p0, p1, p2, p3, g, b, weight, c_ref, l_ref, h_ref, normed, q, k, v, att, lse, sums):
        for i, part in enumerate((p0, p1, p2, p3)):
            rows = slice(i * part_rows, (i + 1) * part_rows)
            normed[rows, :] = (row_norm(part[0].astype(F32)) * g[...] + b[...]).astype(BF)
        for j, target in enumerate((q, k, v)):
            value = dot_nn(normed[...], weight[:, j * width : (j + 1) * width])
            if j == 2:
                target[...] = value.astype(BF)
                continue
            for pair in range(width // lanes):
                columns = slice(pair * lanes, (pair + 1) * lanes)
                target[:, columns] = rope(value[:, columns], c_ref[...], l_ref[...], h_ref[...], 1.0).astype(BF)
        sums[...] = jnp.zeros_like(sums)
        attend_rows(q, k, v, att, sums, length)
        finish_sums(sums, lse)

    part_spec = pl.BlockSpec((1, part_rows, model), lambda *_: (seq, 0, 0))
    table_spec = whole((length, lanes))
    return call(
        kernel,
        (shape((length, model)),) + (shape((length, width)),) * 4 + (shape((8, length), F32),),
        (1,),
        [part_spec] * 4 + [whole((1, model))] * 2 + [whole(w_full.shape)] + [table_spec] * 3,
        (whole((length, model)),) + (whole((length, width)),) * 4 + (whole((8, length)),),
        [pltpu.VMEM((length, lanes), F32)],
        2 * length * model * 3 * width + 4 * length * length * width,
        16_000_000,
        (*parts, gain, shift, w_full, cos, low, high),
    )


PAIRS = {}


def project(rows, w_full, column=0):
    length, width = rows.shape
    half_rows = length // 2
    model = w_full.shape[0]

    def kernel(a, weight, keep, send):
        send[...] = dot_nt(a[half_rows:, :], weight[...]).astype(BF)
        keep[...] = dot_nt(a[:half_rows, :], weight[...]).astype(BF)

    return call(
        kernel,
        (shape((half_rows, model)),) * 2,
        (1,),
        [whole((length, width)), pl.BlockSpec((model, width), lambda *_: (0, column))],
        (whole((half_rows, model)),) * 2,
        [],
        2 * length * width * model,
        length * (width + model) * 2 + model * width * 2,
        (rows, w_full),
    )


def norm_terms(t):
    mean = jnp.mean(t, axis=-1, keepdims=True)
    centred = t - mean
    inv = lax.rsqrt(jnp.mean(centred * centred, axis=-1, keepdims=True) + EPS)
    return centred * inv, inv


def add_terms(refs):
    total = refs[0][...].astype(F32)
    for ref in refs[1:]:
        total = total + ref[...].astype(F32)
    return total


def cross_forward(tokens, seq, terms, norms, weights, kv, valid):
    rows, model = terms[2].shape
    parts = len(weights)
    width = weights[0].shape[1] // 2
    count = kv.shape[3]
    lanes = 2 * HEAD_WIDTH
    heads = width // HEAD_WIDTH
    lse_rows = -(-parts * heads // 8) * 8

    def kernel(t, a, b, c, n_ref, w0, w1, w2, w3, kv_ref, first, second, normed2, normed3, q, att, lse, sums):
        value = t[0].astype(F32) + add_terms((a, b, c))
        first[...] = value
        normed2[...] = (norm_terms(value)[0] * n_ref[1:2, :] + n_ref[4:5, :]).astype(BF)
        sums[...] = jnp.zeros_like(sums)
        total = value
        for p, w in enumerate((w0, w1, w2, w3)):
            columns = pl.ds(p * width, width)
            q[:, columns] = dot_nn(normed2[...], w[:, :width]).astype(BF)
            attend_rows(
                q.at[:, columns], kv_ref.at[p, 0, 0], kv_ref.at[p, 0, 1], att.at[:, columns], sums, valid, p * heads
            )
            total = total + dot_nt(att[:, columns], w[:, width:])
        second[...] = total
        normed3[...] = (norm_terms(total)[0] * n_ref[2:3, :] + n_ref[5:6, :]).astype(BF)
        finish_sums(sums, lse)

    rows_spec = whole((rows, model))
    return call(
        kernel,
        (shape((rows, model), F32),) * 2 + (shape((rows, model)),) * 4 + (shape((lse_rows, rows), F32),),
        (1,),
        [pl.BlockSpec((1, rows, model), lambda *_: (seq, 0, 0))]
        + [rows_spec] * 3
        + [whole(norms.shape)]
        + [whole(weights[0].shape)] * 4
        + [pl.BlockSpec((parts, 1, 2, count, width), lambda *_: (0, seq, 0, 0, 0))],
        (rows_spec,) * 6 + (whole((lse_rows, rows)),),
        [pltpu.VMEM((rows, lanes), F32)],
        4 * rows * model * parts * width + 4 * rows * count * parts * width,
        18_000_000,
        (tokens, *terms, norms, *weights, kv),
    )


def norm_pull(grad, t, gain):
    xhat, inv = norm_terms(t)
    scaled = grad * gain
    back = inv * (
        scaled
        - jnp.mean(scaled, axis=-1, keepdims=True)
        - xhat * jnp.mean(scaled * xhat, axis=-1, keepdims=True)
    )
    return back, jnp.sum(grad * xhat, axis=0, keepdims=True), jnp.sum(grad, axis=0, keepdims=True)


def cross_backward(third, seq, terms, second, first, norms, weights, kv, q, att, lse, valid):
    rows, model = terms[2].shape
    parts = len(weights)
    width = weights[0].shape[1] // 2
    count = kv.shape[3]
    lanes = 2 * HEAD_WIDTH
    heads = width // HEAD_WIDTH

    def kernel(
        t, a, b, c, s_ref, f_ref, n_ref, w0, w1, w2, w3, kv_ref, q_ref, a_ref, l_ref,
        d_first, dy2, dy1, dq, dkv, stats, do, acc,
    ):
        back, gain3, shift3 = norm_pull(add_terms((a, b, c)), s_ref[...], n_ref[2:3, :])
        d_second = t[0].astype(F32) + back
        dy2[...] = d_second.astype(BF)
        d_normed2 = None
        for p, w in enumerate((w0, w1, w2, w3)):
            columns = pl.ds(p * width, width)
            do[...] = dot_nn(dy2[...], w[:, width:]).astype(BF)

            def put_k(rows_at, at, value, p=p):
                dkv[p, 0, rows_at, at] = value.astype(BF)

            def put_v(rows_at, at, value, p=p):
                dkv[p, 1, rows_at, at] = value.astype(BF)

            def put_q(at, value, p=p):
                dq[:, slice(p * width + at.start, p * width + at.stop)] = value.astype(BF)

            attend_back(
                q_ref.at[:, columns], kv_ref.at[p, 0, 0], kv_ref.at[p, 0, 1], a_ref.at[:, columns], do, l_ref, acc,
                put_k, put_v, put_q, valid, p * heads,
            )
            term = dot_nt(dq[:, columns], w[:, :width])
            d_normed2 = term if d_normed2 is None else d_normed2 + term
        back, gain2, shift2 = norm_pull(d_normed2, f_ref[...], n_ref[1:2, :])
        value = d_second + back
        d_first[...] = value
        dy1[...] = value.astype(BF)
        stats[...] = jnp.concatenate([gain2, gain3, shift2, shift3, jnp.zeros((4, model), F32)], axis=0)

    rows_spec = whole((rows, model))
    return call(
        kernel,
        (shape((rows, model), F32),)
        + (shape((rows, model)),) * 3
        + (shape((parts, 2, count, width)), shape((8, model), F32)),
        (1,),
        [pl.BlockSpec((1, rows, model), lambda *_: (seq, 0, 0))]
        + [rows_spec] * 5
        + [whole(norms.shape)]
        + [whole(weights[0].shape)] * 4
        + [pl.BlockSpec((parts, 1, 2, count, width), lambda *_: (0, seq, 0, 0, 0))]
        + [rows_spec] * 2
        + [whole(lse.shape)],
        (rows_spec,) * 4 + (whole((parts, 2, count, width)), whole((8, model))),
        [pltpu.VMEM((rows, width), BF), pltpu.VMEM((rows, lanes), F32)],
        4 * rows * model * parts * width + 10 * rows * count * parts * width,
        24_000_000,
        (third, *terms, second, first, norms, *weights, kv, q, att, lse),
    )


def cross_weight_grad(parity, normed, dys, dqs, atts, parts):
    seqs = len(dys)
    rows, model = dys[0].shape
    width = model // parts
    pairs = PAIRS["pairs"]
    half = model // 2

    def kernel(par, *refs):
        n_refs, y_refs, q_refs, a_refs = (refs[i * seqs : (i + 1) * seqs] for i in range(4))
        outs = refs[4 * seqs : 4 * seqs + parts]
        scr = refs[-1]
        for p in range(parts):
            at = slice(p * width, (p + 1) * width)
            for j, (lefts, rights) in enumerate(((n_refs, q_refs), (y_refs, a_refs))):
                value = None
                for left, right in zip(lefts, rights):
                    term = dot_tn(left[...], right[:, at])
                    value = term if value is None else value + term
                scr[...] = value.astype(BF).reshape(scr.shape)
                columns = slice(j * width, (j + 1) * width)
                outs[p][0, :, columns] = scr[:, pl.ds(par[0], 1)].reshape(half, width)
                outs[p][1, :, columns] = scr[:, pl.ds(1 - par[0], 1)].reshape(half, width)

    return call(
        kernel,
        (shape((2, half, 2 * width)),) * parts,
        (1,),
        [SMEM] + [whole((rows, model))] * (4 * seqs),
        (whole((2, half, 2 * width)),) * parts,
        [pltpu.VMEM((pairs, 2, half // pairs, width), BF)],
        4 * seqs * rows * model * model,
        16_000_000,
        (parity, *normed, *dys, *dqs, *atts),
    )


def gate_forward(parts, weights):
    part_rows, model = parts[0].shape
    length = part_rows * len(parts)
    hidden = weights.shape[2]
    block = 512
    steps = hidden // block

    def kernel(p0, p1, p2, p3, wg, wu, gate, up, act):
        for i, part in enumerate((p0, p1, p2, p3)):
            rows = slice(i * part_rows, (i + 1) * part_rows)
            g = dot_nn(part[...], wg[0])
            u = dot_nn(part[...], wu[0])
            gate[rows, :] = g.astype(BF)
            up[rows, :] = u.astype(BF)
            act[rows, :] = (g / (1.0 + jnp.exp2(-LOG2E * g)) * u).astype(BF)

    g_spec = pl.BlockSpec((1, model, block), lambda j: (0, 0, j))
    u_spec = pl.BlockSpec((1, model, block), lambda j: (1, 0, j))
    out_spec = pl.BlockSpec((length, block), lambda j: (0, j))
    return call(
        kernel,
        (shape((length, hidden)),) * 3,
        (steps,),
        [whole((part_rows, model))] * 4 + [g_spec, u_spec],
        (out_spec,) * 3,
        [],
        4 * length * model * hidden,
        22_000_000,
        (*parts, weights, weights),
    )


def gate_backward(parts, seq, gate, up, w_down, weights):
    part_rows, model = parts[0].shape[1:]
    length = part_rows * len(parts)
    half_rows = length // 2
    hidden = gate.shape[1]
    block = 512
    steps = hidden // block

    def kernel(p0, p1, p2, p3, g_ref, u_ref, wd, wg, wu, dgate, dup, keep, send, acc):
        j = pl.program_id(0)

        @pl.when(j == 0)
        def _():
            acc[...] = jnp.zeros_like(acc)

        for i, part in enumerate((p0, p1, p2, p3)):
            rows = slice(i * part_rows, (i + 1) * part_rows)
            d_hidden = dot_nn(part[0], wd[...])
            g = g_ref[rows, :].astype(F32)
            u = u_ref[rows, :].astype(F32)
            sig = 1.0 / (1.0 + jnp.exp2(-LOG2E * g))
            d_gate = (d_hidden * u * sig * (1.0 + g * (1.0 - sig))).astype(BF)
            d_up = (d_hidden * (g * sig)).astype(BF)
            dgate[rows, :] = d_gate
            dup[rows, :] = d_up
            acc[rows, :] += dot_nt(d_gate, wg[0]) + dot_nt(d_up, wu[0])

        @pl.when(j == steps - 1)
        def _():
            keep[...] = acc[:half_rows, :].astype(BF)
            send[...] = acc[half_rows:, :].astype(BF)

    part_spec = pl.BlockSpec((1, part_rows, model), lambda *_: (seq, 0, 0))
    act_spec = pl.BlockSpec((length, block), lambda j: (0, j))
    w_spec = pl.BlockSpec((model, block), lambda j: (0, j))
    g_spec = pl.BlockSpec((1, model, block), lambda j: (0, 0, j))
    u_spec = pl.BlockSpec((1, model, block), lambda j: (1, 0, j))
    return call(
        kernel,
        (shape((length, hidden)),) * 2 + (shape((half_rows, model)),) * 2,
        (steps,),
        [part_spec] * 4 + [act_spec] * 2 + [w_spec, g_spec, u_spec],
        (act_spec,) * 2 + (whole((half_rows, model)),) * 2,
        [pltpu.VMEM((length, model), F32)],
        6 * length * model * hidden,
        33_000_000,
        (*parts, gate, up, w_down, weights, weights),
    )


def self_backward(parts, o_full, w_full, q, k, v, att, lse, cos, low, high):
    part_rows, model = parts[0].shape
    length = part_rows * len(parts)
    half_rows = length // 2
    width = q.shape[1]
    lanes = 2 * HEAD_WIDTH

    def kernel(
        p0, p1, p2, p3, o_ref, w_ref, q_ref, k_ref, v_ref, a_ref, l_ref, c_ref, lo_ref, h_ref,
        grads, keep, send, do, acc,
    ):
        for i, part in enumerate((p0, p1, p2, p3)):
            do[i * part_rows : (i + 1) * part_rows, :] = dot_nn(part[...], o_ref[...]).astype(BF)

        def put_k(rows, columns, value):
            value = rope(value, c_ref[rows, :], lo_ref[rows, :], h_ref[rows, :], -1.0)
            grads[rows, slice(width + columns.start, width + columns.stop)] = value.astype(BF)

        def put_v(rows, columns, value):
            grads[rows, slice(2 * width + columns.start, 2 * width + columns.stop)] = value.astype(BF)

        def put_q(columns, value):
            grads[:, columns] = rope(value, c_ref[...], lo_ref[...], h_ref[...], -1.0).astype(BF)

        attend_back(q_ref, k_ref, v_ref, a_ref, do, l_ref, acc, put_k, put_v, put_q, length)
        send[...] = dot_nt(grads[half_rows:, :], w_ref[...]).astype(BF)
        keep[...] = dot_nt(grads[:half_rows, :], w_ref[...]).astype(BF)

    o_spec = pl.BlockSpec((model, width), lambda *_: (0, 2))
    rows_spec = whole((length, width))
    return call(
        kernel,
        (shape((length, 3 * width)),) + (shape((half_rows, model)),) * 2,
        (1,),
        [whole((part_rows, model))] * 4
        + [o_spec]
        + [whole(w_full.shape)]
        + [rows_spec] * 4
        + [whole((8, length))]
        + [whole((length, lanes))] * 3,
        (whole((length, 3 * width)),) + (whole((half_rows, model)),) * 2,
        [
            pltpu.VMEM((length, width), BF),
            pltpu.VMEM((length, lanes), F32),
        ],
        8 * length * model * width + 10 * length * length * width,
        24_000_000,
        (*parts, o_full, w_full, q, k, v, att, lse, cos, low, high),
    )


def weight_grad(parity, lefts, rights, block, first=0, steps=None):
    model = lefts[0].shape[-1]
    steps = steps or rights[0].shape[1] // block
    total = steps * block
    pairs = PAIRS["pairs"]
    count = len(lefts)
    half = model // 2
    length = sum(left.shape[0] for left in lefts)

    def kernel(par, *refs):
        left_refs = refs[:count]
        right_refs = refs[count : count + len(rights)]
        own, other, rows_scr, scr = refs[count + len(rights) :]

        @pl.when(pl.program_id(0) == 0)
        def _():
            start = 0
            for left in left_refs:
                rows_scr[start : start + left.shape[0], :] = left[...]
                start += left.shape[0]

        start = 0
        value = None
        for right in right_refs:
            term = dot_tn(rows_scr[start : start + right.shape[0], :], right[...])
            value = term if value is None else value + term
            start += right.shape[0]
        split_rows(par[0], value.astype(BF), scr, own, other, slice(None))

    left_specs = [whole(left.shape) for left in lefts]
    right_specs = [pl.BlockSpec((right.shape[0], block), lambda j: (0, first + j)) for right in rights]
    return call(
        kernel,
        (shape((half, total)),) * 2,
        (steps,),
        [SMEM] + left_specs + right_specs,
        (pl.BlockSpec((half, block), lambda j: (0, j)),) * 2,
        [pltpu.VMEM((length, model), BF), pltpu.VMEM((pairs, 2, model // (2 * pairs), block), BF)],
        2 * length * model * total,
        length * (model + total) * 2 + model * total * 2,
        (parity, *lefts, *rights),
    )


def make_body(dp, group):
    pairs = dp // 2
    swap = [(i, i ^ 1) for i in range(dp)]
    lines = [list(range(0, dp, 2)), list(range(1, dp, 2))]
    over_core = [(i, i ^ 1) for i in range(group)]
    over_x = [(i, i ^ 2) for i in range(group)]

    def body(
        tokens,
        context,
        positions,
        seq_mask,
        cotangent,
        norm_gains,
        norm_shifts,
        w_qkv,
        w_self_out,
        w_cross_q,
        w_cross_kv,
        w_cross_out,
        w_gate_up,
        w_down,
    ):
        PAIRS["pairs"] = pairs
        rank = lax.axis_index("dp")
        spot = lax.axis_index("tensor")
        parity = (rank % 2).astype(jnp.int32).reshape(1)
        seqs, part_rows, model = tokens.shape
        length = positions.shape[1]
        ctx_len = context.shape[1]
        rows = w_qkv.shape[1]
        width = w_qkv.shape[2]
        heads = width // HEAD_WIDTH
        hidden = w_down.shape[0]
        ctx_rows = w_cross_kv.shape[1]

        turns = {}

        def in_turn(axis, v, pairs_of, name):
            if axis in turns:
                v = after(v, turns[axis])
            turns[axis] = lax.ppermute(v, name, pairs_of)
            return turns[axis]

        def fetch_all(local):
            return lax.all_gather(local, "dp", axis=0, tiled=True)

        def pair_sum(own, other, *ready):
            got = in_turn("y", other, swap, "dp")
            return own + after(got, *ready)

        def line_sum(v):
            return lax.psum_scatter(v, "dp", scatter_dimension=0, tiled=True, axis_index_groups=lines).astype(F32)

        def core(v):
            return lax.ppermute(v, "tensor", over_core)

        def across(v):
            return in_turn("x", v, over_x, "tensor")

        def spread(own):
            far = across(own)
            return (own, far, core(own), core(far))

        def reduce_rows(keep, send):
            got = core(send)
            far = (keep[part_rows:].astype(F32) + got[part_rows:].astype(F32)).astype(BF)
            return keep, got, across(far)

        def gather_sum(keep, got, back):
            return keep[:part_rows].astype(F32) + got[:part_rows].astype(F32) + back.astype(F32)

        def reduce_parts(own, far, near, both):
            own = (own.astype(F32) + core(near).astype(F32)).astype(BF)
            far = (far.astype(F32) + core(both).astype(F32)).astype(BF)
            return own, across(far)

        def total_of(v):
            v = v + lax.ppermute(v, "tensor", over_core)
            for bit in range((dp - 1).bit_length()):
                v = v + lax.ppermute(v, "dp", [(i, i ^ (1 << bit)) for i in range(dp)])
            return v + across(v)

        order = jnp.stack([spot, spot ^ 2, spot ^ 1, spot ^ 3])
        half_rot = ROT // 2
        lane = jnp.arange(2 * HEAD_WIDTH) % HEAD_WIDTH
        inverse = jnp.exp((lane % half_rot).astype(F32) * (-2.0 * math.log(10000.0) / ROT))
        tables = []
        for s in range(seqs):
            spots = jnp.take(positions[s].reshape(group, part_rows), order, axis=0).reshape(length)
            angles = spots.astype(F32)[:, None] * inverse[None, :]
            turned = lane < ROT
            sine = jnp.sin(angles)
            tables.append(
                (
                    jnp.where(turned, jnp.cos(angles), 1.0),
                    jnp.where(lane < half_rot, sine, 0.0),
                    jnp.where((lane >= half_rot) & turned, sine, 0.0),
                )
            )

        place = rank * group + spot
        mine = jnp.concatenate([norm_gains, norm_shifts], axis=0)
        share = mine.shape[1]
        token_parts = spread(tokens)
        norms = total_of(lax.dynamic_update_slice(jnp.zeros((6, model), F32), mine, (0, place * share)))
        gains = [norms[j : j + 1] for j in range(3)]
        shifts = [norms[3 + j : 4 + j] for j in range(3)]
        keep_scale = seq_mask.astype(F32)[:, None, None]
        grad_third = cotangent.astype(F32) * keep_scale
        third_parts = spread(grad_third.astype(BF))

        w_one = jnp.transpose(w_qkv, (1, 0, 2)).reshape(rows, 3 * width)
        qkv_full = fetch_all(w_one)
        w_two = jnp.concatenate(
            [w_cross_q, w_cross_out.T, w_self_out.T, w_cross_kv.reshape(rows, width)], axis=1
        )
        two_full = fetch_all(after(w_two, qkv_full, token_parts[1], tables[0][0], norms))

        state = [dict() for _ in range(seqs)]
        for s in range(seqs):
            st = state[s]
            gain = gains[0]
            if s > 0:
                gain = after(gain, state[0]["att"], third_parts[1])
            st["normed1"], st["q"], st["k"], st["v"], st["att"], st["lse"] = self_forward(
                token_parts, s, gain, shifts[0], qkv_full, *tables[s], heads
            )
        last = state[seqs - 1]["att"]
        two_full = after(two_full, last)
        gu_full = lax.all_gather(after(w_gate_up, two_full), "dp", axis=1, tiled=True)
        cross_parts = spread(two_full[:, : 2 * width])

        ctx_pad = -(-ctx_len // 128) * 128
        kv_weight = jnp.transpose(two_full[:, 3 * width :].reshape(dp, 2, ctx_rows, width), (1, 0, 2, 3))
        kv_weight = kv_weight.reshape(2, dp * ctx_rows, width)
        cross_kv = jnp.einsum("scd,kdh->skch", context, kv_weight, preferred_element_type=F32).astype(BF)
        cross_kv = jnp.stack(spread(cross_kv))
        cross_kv = jnp.pad(cross_kv, ((0, 0), (0, 0), (0, 0), (0, ctx_pad - ctx_len), (0, 0)))

        for s in range(seqs):
            st = state[s]
            st["terms"] = reduce_rows(*project(after(st["att"], last), two_full, 2))
            last = st["terms"][0]
        for s in range(seqs):
            st = state[s]
            terms = st["terms"]
            if s > 0:
                terms = (after(terms[0], state[s - 1]["second"]), *terms[1:])
            st["first"], st["second"], st["normed2"], normed3, st["cq"], st["crossed"], st["clse"] = cross_forward(
                tokens, s, terms, norms, cross_parts, cross_kv, ctx_len
            )
            st["normed3"] = spread(normed3)
        dn_full = fetch_all(after(w_down.T, gu_full, *(st["normed3"][0] for st in state)))
        for s in range(seqs):
            st = state[s]
            st["gate"], st["up"], st["hidden"] = gate_forward(st["normed3"], gu_full)
        third_lefts = [part[s] for s in range(seqs) for part in third_parts]
        dn_pair = weight_grad(parity, third_lefts, [st["hidden"] for st in state], 384)
        last = dn_pair[1]
        for s in range(seqs):
            st = state[s]
            st["dgate"], st["dup"], keep, send = gate_backward(
                third_parts, s, after(st["gate"], last), st["up"], dn_full, gu_full
            )
            last = keep
            st["d_normed3"] = reduce_rows(keep, send)
        dn_sum = pair_sum(*dn_pair, last)
        dn_grad = line_sum(dn_sum)
        normed3 = [p for st in state for p in st["normed3"]]
        gate_pair = weight_grad(parity, normed3, [after(st["dgate"], dn_sum) for st in state], 384)
        up_pair = weight_grad(parity, normed3, [after(st["dup"], gate_pair[1]) for st in state], 384)

        gain_grads, shift_grads = [0.0] * 3, [0.0] * 3
        last = up_pair[1]
        for s in range(seqs):
            st = state[s]
            st["d_first"], st["dy2"], dy1, st["dcq"], st["dkv"], stats = cross_backward(
                third_parts[0], s, st["d_normed3"], st["second"], after(st["first"], last), norms, cross_parts,
                cross_kv, st["cq"], st["crossed"], st["clse"], ctx_len,
            )
            last = dy1
            for j in range(1, 3):
                gain_grads[j] += stats[j - 1]
                shift_grads[j] += stats[j + 1]
            st["dy1"] = spread(dy1)
        gate_sum = pair_sum(*gate_pair, last)
        gate_part = line_sum(after(gate_sum, dn_grad))
        cross_terms = cross_weight_grad(
            parity,
            [after(st["normed2"], last, state[0]["dy1"][1]) for st in state],
            [st["dy2"] for st in state],
            [st["dcq"] for st in state],
            [st["crossed"] for st in state],
            group,
        )
        up_other = after(up_pair[1], last)
        last = cross_terms[0]
        for s in range(seqs):
            st = state[s]
            st["out_terms"] = project(after(st["hidden"], last), dn_full)
            last = st["out_terms"][0]
        dkv_own, dkv_far = reduce_parts(*(jnp.stack([st["dkv"][p] for st in state]) for p in range(group)))
        cross_mine, cross_far = reduce_parts(*cross_terms)
        last = (last, dn_grad, gate_sum, *(p for st in state for p in st["dy1"]))
        for s in range(seqs):
            st = state[s]
            st["dqkv"], keep, send = self_backward(
                st["dy1"], two_full, qkv_full,
                after(st["q"], *last), st["k"], st["v"], st["att"], st["lse"], *tables[s],
            )
            last = keep
            st["d_normed1"] = (keep, send)
            if s > 0:
                continue
            up_sum = pair_sum(up_pair[0], up_other, last)
            up_part = line_sum(after(up_sum, gate_part))
            so_pair = weight_grad(
                parity,
                [p for st in state for p in st["dy1"]],
                [after(st["att"], last, gate_part) for st in state],
                width,
            )
            dkv = (dkv_own.astype(F32) + after(dkv_far, last).astype(F32)).astype(BF)[:, :, :ctx_len]
            kv_grad = jnp.einsum("scd,skch->kdh", context, dkv, preferred_element_type=F32).astype(BF)
            kv_grad = jnp.transpose(kv_grad.reshape(2, pairs, 2, ctx_rows, width), (1, 2, 0, 3, 4))
            even = parity[0] == 0
            kv_mine = jnp.where(even, kv_grad[:, 0], kv_grad[:, 1]).reshape(pairs * rows, width)
            kv_other = jnp.where(even, kv_grad[:, 1], kv_grad[:, 0]).reshape(pairs * rows, width)
            cross_sum = cross_mine + after(cross_far, so_pair)
            middle_pair = [
                jnp.concatenate(v, axis=1)
                for v in ((cross_sum[0], kv_mine, so_pair[0]), (cross_sum[1], kv_other, so_pair[1]))
            ]
            last = (up_sum, *middle_pair)
        middle_sum = pair_sum(*middle_pair, keep)
        normed1 = [st["normed1"] for st in state]
        qkv_pair = weight_grad(
            parity, normed1, [after(st["dqkv"], up_part) for st in state], width
        )
        middle = line_sum(after(middle_sum, up_part))
        for st in state:
            st["out_terms"] = reduce_rows(*st["out_terms"])
        for st in state:
            st["d_normed1"] = reduce_rows(*st["d_normed1"])
        qkv_part = line_sum(after(pair_sum(*qkv_pair, state[0]["d_normed1"][2]), middle))
        outs = []
        for s in range(seqs):
            st = state[s]
            third = st["second"] + gather_sum(*st["out_terms"])
            outs.append((third * keep_scale[s]).astype(BF))
        grad_inputs = []
        for s in range(seqs):
            st = state[s]
            xhat, inv = norm_parts(tokens[s].astype(F32))
            back, gain_term, shift_term = norm_back(
                gather_sum(*(after(v, qkv_pair[1]) for v in st["d_normed1"])), xhat, inv, gains[0]
            )
            gain_grads[0] += gain_term
            shift_grads[0] += shift_term
            grad_inputs.append(st["d_first"] + back)
        norm_grads = lax.dynamic_slice(
            total_of(jnp.stack(gain_grads + shift_grads)), (0, place * share), (6, share)
        )
        return (
            jnp.stack(outs),
            jnp.stack(grad_inputs),
            norm_grads[:3],
            norm_grads[3:],
            jnp.transpose(qkv_part.reshape(rows, 3, width), (1, 0, 2)),
            middle[:, 3 * width :].T,
            middle[:, :width],
            middle[:, 2 * width : 3 * width].reshape(2, ctx_rows, width),
            middle[:, width : 2 * width].T,
            jnp.stack([gate_part, up_part]),
            dn_grad.T,
        )

    return body


def norm_parts(rows):
    mean = jnp.mean(rows, axis=-1, keepdims=True)
    centred = rows - mean
    inv = lax.rsqrt(jnp.mean(centred * centred, axis=-1, keepdims=True) + EPS)
    return centred * inv, inv


def norm_back(grad, xhat, inv, gain):
    scaled = grad * gain
    back = inv * (
        scaled
        - jnp.mean(scaled, axis=-1, keepdims=True)
        - xhat * jnp.mean(scaled * xhat, axis=-1, keepdims=True)
    )
    return back, jnp.sum(grad * xhat, axis=0), jnp.sum(grad, axis=0)


def solution(mesh):
    in_specs = (
        P("dp", "tensor", None),
        P("dp", None, None),
        P("dp", None),
        P("dp"),
        P("dp", "tensor", None),
        P(None, ("dp", "tensor")),
        P(None, ("dp", "tensor")),
        P(None, "dp", "tensor"),
        P("tensor", "dp"),
        P("dp", "tensor"),
        P(None, "dp", "tensor"),
        P("tensor", "dp"),
        P(None, "dp", "tensor"),
        P("tensor", "dp"),
    )
    out_specs = (
        P("dp", "tensor", None),
        P("dp", "tensor", None),
        P(None, ("dp", "tensor")),
        P(None, ("dp", "tensor")),
        P(None, "dp", "tensor"),
        P("tensor", "dp"),
        P("dp", "tensor"),
        P(None, "dp", "tensor"),
        P("tensor", "dp"),
        P(None, "dp", "tensor"),
        P("tensor", "dp"),
    )
    body = make_body(mesh.shape["dp"], mesh.shape["tensor"])
    return jax.shard_map(body, mesh=mesh, in_specs=in_specs, out_specs=out_specs, check_vma=False)
```

```python
import functools
import math

import jax
import jax.numpy as jnp
from jax import lax
from jax.experimental import pallas as pl
from jax.experimental.pallas import tpu as pltpu
from jax.sharding import PartitionSpec as P

HEAD_WIDTH = 64
ROT = 32
EPS = 1e-05
BF = jnp.bfloat16
F32 = jnp.float32
LOG2E = math.log2(math.e)
VMEM_BYTES = 56 * 1024 * 1024


def call(kernel, outs, grid, in_specs, out_specs, scratch, flops, moved, operands):
    return pl.pallas_call(
        kernel,
        out_shape=outs,
        grid=grid,
        in_specs=in_specs,
        out_specs=out_specs,
        scratch_shapes=scratch,
        compiler_params=pltpu.CompilerParams(vmem_limit_bytes=VMEM_BYTES),
        cost_estimate=pl.CostEstimate(flops=flops * 3, bytes_accessed=moved, transcendentals=0),
    )(*operands)


def after(value, *others):
    return lax.optimization_barrier((value, *others))[0]


def shape(dims, kind=BF):
    return jax.ShapeDtypeStruct(dims, kind)


def whole(dims):
    return pl.BlockSpec(dims, lambda *_: (0,) * len(dims))


SMEM = pl.BlockSpec(memory_space=pltpu.SMEM)


def dot_nn(a, b):
    return jnp.dot(a, b, preferred_element_type=F32)


def dot_nt(a, b):
    return lax.dot_general(a, b, (((1,), (1,)), ((), ())), preferred_element_type=F32)


def dot_tn(a, b):
    return lax.dot_general(a, b, (((0,), (0,)), ((), ())), preferred_element_type=F32)


def assemble(parity, own, other, scratch):
    pairs, _, rows, width = scratch.shape
    scratch[:, pl.ds(parity, 1)] = own[...].reshape(pairs, 1, rows, width)
    scratch[:, pl.ds(1 - parity, 1)] = other[...].reshape(pairs, 1, rows, width)
    return scratch[...].reshape(pairs * 2 * rows, width)


def split_rows(parity, value, scratch, own, other, columns):
    pairs, _, rows, width = scratch.shape
    scratch[...] = value.reshape(scratch.shape)
    own[:, columns] = scratch[:, pl.ds(parity, 1)].reshape(pairs * rows, width)
    other[:, columns] = scratch[:, pl.ds(1 - parity, 1)].reshape(pairs * rows, width)


def rope(v, cosine, low_sine, high_sine, sign):
    width = v.shape[-1]
    half = ROT // 2
    ahead = pltpu.roll(v, width - half, 1)
    behind = pltpu.roll(v, half, 1)
    return v * cosine + sign * (behind * high_sine - ahead * low_sine)


def head_mask(h):
    lane = lax.broadcasted_iota(jnp.int32, (1, 2 * HEAD_WIDTH), 1)
    return (lane // HEAD_WIDTH) == h


def attend_rows(q_ref, k_ref, v_ref, att_ref, lse_scratch, valid, base=0):
    length, width = q_ref.shape
    keys = k_ref.shape[0]
    block = min(256, length)
    scale = HEAD_WIDTH**-0.5 * LOG2E
    lanes = 2 * HEAD_WIDTH

    def rows_step(i, _):
        rows = pl.ds(pl.multiple_of(i * block, block), block)
        lane = lax.broadcasted_iota(jnp.int32, (block, lanes), 1)
        sums = lse_scratch[rows, :]
        for pair in range(width // lanes):
            columns = slice(pair * lanes, (pair + 1) * lanes)
            q = q_ref[rows, columns]
            total = None
            for h in range(2):
                mask = head_mask(h)
                k = jnp.where(mask, k_ref[:, columns], jnp.zeros((), BF))
                v = jnp.where(mask, v_ref[:, columns], jnp.zeros((), BF))
                logits = dot_nt(q, k) * scale
                if valid < keys:
                    spot = lax.broadcasted_iota(jnp.int32, logits.shape, 1)
                    logits = jnp.where(spot < valid, logits, -jnp.inf)
                peak = jnp.max(logits, axis=1, keepdims=True)
                weights = jnp.exp2(logits - peak)
                norm = jnp.sum(weights, axis=1, keepdims=True)
                term = dot_nn(weights.astype(BF), v) / norm
                total = term if total is None else total + term
                sums = jnp.where(lane == base + pair * 2 + h, peak + jnp.log2(norm), sums)
            att_ref[rows, columns] = total.astype(BF)
        lse_scratch[rows, :] = sums
        return 0

    lax.fori_loop(0, length // block, rows_step, 0)


def attend_back(q_ref, k_ref, v_ref, att_ref, do_ref, lse_ref, dq_acc, put_k, put_v, put_q, valid, base=0):
    length, width = q_ref.shape
    keys = k_ref.shape[0]
    block = min(256, keys)
    scale = HEAD_WIDTH**-0.5
    lanes = 2 * HEAD_WIDTH
    for pair in range(width // lanes):
        columns = slice(pair * lanes, (pair + 1) * lanes)
        product = do_ref[:, columns].astype(F32) * att_ref[:, columns].astype(F32)
        deltas = []
        for h in range(2):
            ones = jnp.where(head_mask(h), 1.0, 0.0).astype(F32)
            deltas.append(
                lax.dot_general(
                    jnp.broadcast_to(ones, (8, lanes)),
                    product,
                    (((1,), (1,)), ((), ())),
                    preferred_element_type=F32,
                    precision=lax.Precision.HIGHEST,
                )[:1]
            )
        dq_acc[...] = jnp.zeros_like(dq_acc)

        def keys_step(i, _):
            rows = pl.ds(pl.multiple_of(i * block, block), block)
            dk_total, dv_total = None, None
            for h in range(2):
                mask = head_mask(h)
                zero = jnp.zeros((), BF)
                k = jnp.where(mask, k_ref[rows, columns], zero)
                v = jnp.where(mask, v_ref[rows, columns], zero)
                q = q_ref[:, columns]
                do = do_ref[:, columns]
                head = base + pair * 2 + h
                logits = dot_nt(k, q) * (scale * LOG2E)
                weights = jnp.exp2(logits - lse_ref[head : head + 1, :])
                if valid < keys:
                    spot = i * block + lax.broadcasted_iota(jnp.int32, weights.shape, 0)
                    weights = jnp.where(spot < valid, weights, 0.0)
                dp = dot_nt(v, do)
                ds = (weights * (dp - deltas[h])).astype(BF)
                dv = dot_nn(weights.astype(BF), jnp.where(mask, do, zero))
                dk = dot_nn(ds, jnp.where(mask, q, zero))
                dq_acc[...] += dot_tn(ds, k)
                dk_total = dk if dk_total is None else dk_total + dk
                dv_total = dv if dv_total is None else dv_total + dv
            put_k(rows, columns, dk_total * scale)
            put_v(rows, columns, dv_total)
            return 0

        lax.fori_loop(0, keys // block, keys_step, 0)
        put_q(columns, dq_acc[...] * scale)


def finish_sums(lse_scratch, lse_ref):
    lse_ref[...] = jnp.transpose(lse_scratch[...])[: lse_ref.shape[0]]


def row_norm(t):
    mean = jnp.mean(t, axis=-1, keepdims=True)
    centred = t - mean
    return centred * lax.rsqrt(jnp.mean(centred * centred, axis=-1, keepdims=True) + EPS)


def self_forward(parts, seq, gain, shift, w_full, cos, low, high, heads):
    part_rows, model = parts[0].shape[1:]
    length = part_rows * len(parts)
    width = heads * HEAD_WIDTH
    lanes = 2 * HEAD_WIDTH

    def kernel(p0, p1, p2, p3, g, b, weight, c_ref, l_ref, h_ref, normed, q, k, v, att, lse, sums):
        for i, part in enumerate((p0, p1, p2, p3)):
            rows = slice(i * part_rows, (i + 1) * part_rows)
            normed[rows, :] = (row_norm(part[0].astype(F32)) * g[...] + b[...]).astype(BF)
        for j, target in enumerate((q, k, v)):
            value = dot_nn(normed[...], weight[:, j * width : (j + 1) * width])
            if j == 2:
                target[...] = value.astype(BF)
                continue
            for pair in range(width // lanes):
                columns = slice(pair * lanes, (pair + 1) * lanes)
                target[:, columns] = rope(value[:, columns], c_ref[...], l_ref[...], h_ref[...], 1.0).astype(BF)
        sums[...] = jnp.zeros_like(sums)
        attend_rows(q, k, v, att, sums, length)
        finish_sums(sums, lse)

    part_spec = pl.BlockSpec((1, part_rows, model), lambda *_: (seq, 0, 0))
    table_spec = whole((length, lanes))
    return call(
        kernel,
        (shape((length, model)),) + (shape((length, width)),) * 4 + (shape((8, length), F32),),
        (1,),
        [part_spec] * 4 + [whole((1, model))] * 2 + [whole(w_full.shape)] + [table_spec] * 3,
        (whole((length, model)),) + (whole((length, width)),) * 4 + (whole((8, length)),),
        [pltpu.VMEM((length, lanes), F32)],
        2 * length * model * 3 * width + 4 * length * length * width,
        16_000_000,
        (*parts, gain, shift, w_full, cos, low, high),
    )


PAIRS = {}


def project(rows, w_full, column=0):
    length, width = rows.shape
    half_rows = length // 2
    model = w_full.shape[0]

    def kernel(a, weight, keep, send):
        send[...] = dot_nt(a[half_rows:, :], weight[...]).astype(BF)
        keep[...] = dot_nt(a[:half_rows, :], weight[...]).astype(BF)

    return call(
        kernel,
        (shape((half_rows, model)),) * 2,
        (1,),
        [whole((length, width)), pl.BlockSpec((model, width), lambda *_: (0, column))],
        (whole((half_rows, model)),) * 2,
        [],
        2 * length * width * model,
        length * (width + model) * 2 + model * width * 2,
        (rows, w_full),
    )


def norm_terms(t):
    mean = jnp.mean(t, axis=-1, keepdims=True)
    centred = t - mean
    inv = lax.rsqrt(jnp.mean(centred * centred, axis=-1, keepdims=True) + EPS)
    return centred * inv, inv


def add_terms(refs):
    total = refs[0][...].astype(F32)
    for ref in refs[1:]:
        total = total + ref[...].astype(F32)
    return total


def cross_forward(tokens, seq, terms, norms, weights, kv, valid):
    rows, model = terms[2].shape
    parts = len(weights)
    width = weights[0].shape[1] // 2
    count = kv.shape[3]
    lanes = 2 * HEAD_WIDTH
    heads = width // HEAD_WIDTH
    lse_rows = -(-parts * heads // 8) * 8

    def kernel(t, a, b, c, n_ref, w0, w1, w2, w3, kv_ref, first, second, normed2, normed3, q, att, lse, sums):
        value = t[0].astype(F32) + add_terms((a, b, c))
        first[...] = value
        normed2[...] = (norm_terms(value)[0] * n_ref[1:2, :] + n_ref[4:5, :]).astype(BF)
        sums[...] = jnp.zeros_like(sums)
        total = value
        for p, w in enumerate((w0, w1, w2, w3)):
            columns = pl.ds(p * width, width)
            q[:, columns] = dot_nn(normed2[...], w[:, :width]).astype(BF)
            attend_rows(
                q.at[:, columns], kv_ref.at[p, 0, 0], kv_ref.at[p, 0, 1], att.at[:, columns], sums, valid, p * heads
            )
            total = total + dot_nt(att[:, columns], w[:, width:])
        second[...] = total
        normed3[...] = (norm_terms(total)[0] * n_ref[2:3, :] + n_ref[5:6, :]).astype(BF)
        finish_sums(sums, lse)

    rows_spec = whole((rows, model))
    return call(
        kernel,
        (shape((rows, model), F32),) * 2 + (shape((rows, model)),) * 4 + (shape((lse_rows, rows), F32),),
        (1,),
        [pl.BlockSpec((1, rows, model), lambda *_: (seq, 0, 0))]
        + [rows_spec] * 3
        + [whole(norms.shape)]
        + [whole(weights[0].shape)] * 4
        + [pl.BlockSpec((parts, 1, 2, count, width), lambda *_: (0, seq, 0, 0, 0))],
        (rows_spec,) * 6 + (whole((lse_rows, rows)),),
        [pltpu.VMEM((rows, lanes), F32)],
        4 * rows * model * parts * width + 4 * rows * count * parts * width,
        18_000_000,
        (tokens, *terms, norms, *weights, kv),
    )


def norm_pull(grad, t, gain):
    xhat, inv = norm_terms(t)
    scaled = grad * gain
    back = inv * (
        scaled
        - jnp.mean(scaled, axis=-1, keepdims=True)
        - xhat * jnp.mean(scaled * xhat, axis=-1, keepdims=True)
    )
    return back, jnp.sum(grad * xhat, axis=0, keepdims=True), jnp.sum(grad, axis=0, keepdims=True)


def cross_backward(third, seq, terms, second, first, norms, weights, kv, q, att, lse, valid):
    rows, model = terms[2].shape
    parts = len(weights)
    width = weights[0].shape[1] // 2
    count = kv.shape[3]
    lanes = 2 * HEAD_WIDTH
    heads = width // HEAD_WIDTH

    def kernel(
        t, a, b, c, s_ref, f_ref, n_ref, w0, w1, w2, w3, kv_ref, q_ref, a_ref, l_ref,
        d_first, dy2, dy1, dq, dkv, stats, do, acc,
    ):
        back, gain3, shift3 = norm_pull(add_terms((a, b, c)), s_ref[...], n_ref[2:3, :])
        d_second = t[0].astype(F32) + back
        dy2[...] = d_second.astype(BF)
        d_normed2 = None
        for p, w in enumerate((w0, w1, w2, w3)):
            columns = pl.ds(p * width, width)
            do[...] = dot_nn(dy2[...], w[:, width:]).astype(BF)

            def put_k(rows_at, at, value, p=p):
                dkv[p, 0, rows_at, at] = value.astype(BF)

            def put_v(rows_at, at, value, p=p):
                dkv[p, 1, rows_at, at] = value.astype(BF)

            def put_q(at, value, p=p):
                dq[:, slice(p * width + at.start, p * width + at.stop)] = value.astype(BF)

            attend_back(
                q_ref.at[:, columns], kv_ref.at[p, 0, 0], kv_ref.at[p, 0, 1], a_ref.at[:, columns], do, l_ref, acc,
                put_k, put_v, put_q, valid, p * heads,
            )
            term = dot_nt(dq[:, columns], w[:, :width])
            d_normed2 = term if d_normed2 is None else d_normed2 + term
        back, gain2, shift2 = norm_pull(d_normed2, f_ref[...], n_ref[1:2, :])
        value = d_second + back
        d_first[...] = value
        dy1[...] = value.astype(BF)
        stats[...] = jnp.concatenate([gain2, gain3, shift2, shift3, jnp.zeros((4, model), F32)], axis=0)

    rows_spec = whole((rows, model))
    return call(
        kernel,
        (shape((rows, model), F32),)
        + (shape((rows, model)),) * 3
        + (shape((parts, 2, count, width)), shape((8, model), F32)),
        (1,),
        [pl.BlockSpec((1, rows, model), lambda *_: (seq, 0, 0))]
        + [rows_spec] * 5
        + [whole(norms.shape)]
        + [whole(weights[0].shape)] * 4
        + [pl.BlockSpec((parts, 1, 2, count, width), lambda *_: (0, seq, 0, 0, 0))]
        + [rows_spec] * 2
        + [whole(lse.shape)],
        (rows_spec,) * 4 + (whole((parts, 2, count, width)), whole((8, model))),
        [pltpu.VMEM((rows, width), BF), pltpu.VMEM((rows, lanes), F32)],
        4 * rows * model * parts * width + 10 * rows * count * parts * width,
        24_000_000,
        (third, *terms, second, first, norms, *weights, kv, q, att, lse),
    )


def cross_weight_grad(parity, normed, dys, dqs, atts, parts):
    seqs = len(dys)
    rows, model = dys[0].shape
    width = model // parts
    pairs = PAIRS["pairs"]
    half = model // 2

    def kernel(par, *refs):
        n_refs, y_refs, q_refs, a_refs = (refs[i * seqs : (i + 1) * seqs] for i in range(4))
        outs = refs[4 * seqs : 4 * seqs + parts]
        scr = refs[-1]
        for p in range(parts):
            at = slice(p * width, (p + 1) * width)
            for j, (lefts, rights) in enumerate(((n_refs, q_refs), (y_refs, a_refs))):
                value = None
                for left, right in zip(lefts, rights):
                    term = dot_tn(left[...], right[:, at])
                    value = term if value is None else value + term
                scr[...] = value.astype(BF).reshape(scr.shape)
                columns = slice(j * width, (j + 1) * width)
                outs[p][0, :, columns] = scr[:, pl.ds(par[0], 1)].reshape(half, width)
                outs[p][1, :, columns] = scr[:, pl.ds(1 - par[0], 1)].reshape(half, width)

    return call(
        kernel,
        (shape((2, half, 2 * width)),) * parts,
        (1,),
        [SMEM] + [whole((rows, model))] * (4 * seqs),
        (whole((2, half, 2 * width)),) * parts,
        [pltpu.VMEM((pairs, 2, half // pairs, width), BF)],
        4 * seqs * rows * model * model,
        16_000_000,
        (parity, *normed, *dys, *dqs, *atts),
    )


def gate_forward(parts, weights):
    part_rows, model = parts[0].shape
    length = part_rows * len(parts)
    hidden = weights.shape[2]
    block = 512
    steps = hidden // block

    def kernel(p0, p1, p2, p3, wg, wu, gate, up, act):
        for i, part in enumerate((p0, p1, p2, p3)):
            rows = slice(i * part_rows, (i + 1) * part_rows)
            g = dot_nn(part[...], wg[0])
            u = dot_nn(part[...], wu[0])
            gate[rows, :] = g.astype(BF)
            up[rows, :] = u.astype(BF)
            act[rows, :] = (g / (1.0 + jnp.exp2(-LOG2E * g)) * u).astype(BF)

    g_spec = pl.BlockSpec((1, model, block), lambda j: (0, 0, j))
    u_spec = pl.BlockSpec((1, model, block), lambda j: (1, 0, j))
    out_spec = pl.BlockSpec((length, block), lambda j: (0, j))
    return call(
        kernel,
        (shape((length, hidden)),) * 3,
        (steps,),
        [whole((part_rows, model))] * 4 + [g_spec, u_spec],
        (out_spec,) * 3,
        [],
        4 * length * model * hidden,
        22_000_000,
        (*parts, weights, weights),
    )


def gate_backward(parts, seq, gate, up, w_down, weights):
    part_rows, model = parts[0].shape[1:]
    length = part_rows * len(parts)
    half_rows = length // 2
    hidden = gate.shape[1]
    block = 512
    steps = hidden // block

    def kernel(p0, p1, p2, p3, g_ref, u_ref, wd, wg, wu, dgate, dup, keep, send, acc):
        j = pl.program_id(0)

        @pl.when(j == 0)
        def _():
            acc[...] = jnp.zeros_like(acc)

        for i, part in enumerate((p0, p1, p2, p3)):
            rows = slice(i * part_rows, (i + 1) * part_rows)
            d_hidden = dot_nn(part[0], wd[...])
            g = g_ref[rows, :].astype(F32)
            u = u_ref[rows, :].astype(F32)
            sig = 1.0 / (1.0 + jnp.exp2(-LOG2E * g))
            d_gate = (d_hidden * u * sig * (1.0 + g * (1.0 - sig))).astype(BF)
            d_up = (d_hidden * (g * sig)).astype(BF)
            dgate[rows, :] = d_gate
            dup[rows, :] = d_up
            acc[rows, :] += dot_nt(d_gate, wg[0]) + dot_nt(d_up, wu[0])

        @pl.when(j == steps - 1)
        def _():
            keep[...] = acc[:half_rows, :].astype(BF)
            send[...] = acc[half_rows:, :].astype(BF)

    part_spec = pl.BlockSpec((1, part_rows, model), lambda *_: (seq, 0, 0))
    act_spec = pl.BlockSpec((length, block), lambda j: (0, j))
    w_spec = pl.BlockSpec((model, block), lambda j: (0, j))
    g_spec = pl.BlockSpec((1, model, block), lambda j: (0, 0, j))
    u_spec = pl.BlockSpec((1, model, block), lambda j: (1, 0, j))
    return call(
        kernel,
        (shape((length, hidden)),) * 2 + (shape((half_rows, model)),) * 2,
        (steps,),
        [part_spec] * 4 + [act_spec] * 2 + [w_spec, g_spec, u_spec],
        (act_spec,) * 2 + (whole((half_rows, model)),) * 2,
        [pltpu.VMEM((length, model), F32)],
        6 * length * model * hidden,
        33_000_000,
        (*parts, gate, up, w_down, weights, weights),
    )


def self_backward(parts, o_full, w_full, q, k, v, att, lse, cos, low, high):
    part_rows, model = parts[0].shape
    length = part_rows * len(parts)
    half_rows = length // 2
    width = q.shape[1]
    lanes = 2 * HEAD_WIDTH

    def kernel(
        p0, p1, p2, p3, o_ref, w_ref, q_ref, k_ref, v_ref, a_ref, l_ref, c_ref, lo_ref, h_ref,
        grads, keep, send, do, acc,
    ):
        for i, part in enumerate((p0, p1, p2, p3)):
            do[i * part_rows : (i + 1) * part_rows, :] = dot_nn(part[...], o_ref[...]).astype(BF)

        def put_k(rows, columns, value):
            value = rope(value, c_ref[rows, :], lo_ref[rows, :], h_ref[rows, :], -1.0)
            grads[rows, slice(width + columns.start, width + columns.stop)] = value.astype(BF)

        def put_v(rows, columns, value):
            grads[rows, slice(2 * width + columns.start, 2 * width + columns.stop)] = value.astype(BF)

        def put_q(columns, value):
            grads[:, columns] = rope(value, c_ref[...], lo_ref[...], h_ref[...], -1.0).astype(BF)

        attend_back(q_ref, k_ref, v_ref, a_ref, do, l_ref, acc, put_k, put_v, put_q, length)
        send[...] = dot_nt(grads[half_rows:, :], w_ref[...]).astype(BF)
        keep[...] = dot_nt(grads[:half_rows, :], w_ref[...]).astype(BF)

    o_spec = pl.BlockSpec((model, width), lambda *_: (0, 2))
    rows_spec = whole((length, width))
    return call(
        kernel,
        (shape((length, 3 * width)),) + (shape((half_rows, model)),) * 2,
        (1,),
        [whole((part_rows, model))] * 4
        + [o_spec]
        + [whole(w_full.shape)]
        + [rows_spec] * 4
        + [whole((8, length))]
        + [whole((length, lanes))] * 3,
        (whole((length, 3 * width)),) + (whole((half_rows, model)),) * 2,
        [
            pltpu.VMEM((length, width), BF),
            pltpu.VMEM((length, lanes), F32),
        ],
        8 * length * model * width + 10 * length * length * width,
        24_000_000,
        (*parts, o_full, w_full, q, k, v, att, lse, cos, low, high),
    )


def weight_grad(parity, lefts, rights, block, first=0, steps=None):
    model = lefts[0].shape[-1]
    steps = steps or rights[0].shape[1] // block
    total = steps * block
    pairs = PAIRS["pairs"]
    count = len(lefts)
    half = model // 2
    length = sum(left.shape[0] for left in lefts)

    def kernel(par, *refs):
        left_refs = refs[:count]
        right_refs = refs[count : count + len(rights)]
        own, other, rows_scr, scr = refs[count + len(rights) :]

        @pl.when(pl.program_id(0) == 0)
        def _():
            start = 0
            for left in left_refs:
                rows_scr[start : start + left.shape[0], :] = left[...]
                start += left.shape[0]

        start = 0
        value = None
        for right in right_refs:
            term = dot_tn(rows_scr[start : start + right.shape[0], :], right[...])
            value = term if value is None else value + term
            start += right.shape[0]
        split_rows(par[0], value.astype(BF), scr, own, other, slice(None))

    left_specs = [whole(left.shape) for left in lefts]
    right_specs = [pl.BlockSpec((right.shape[0], block), lambda j: (0, first + j)) for right in rights]
    return call(
        kernel,
        (shape((half, total)),) * 2,
        (steps,),
        [SMEM] + left_specs + right_specs,
        (pl.BlockSpec((half, block), lambda j: (0, j)),) * 2,
        [pltpu.VMEM((length, model), BF), pltpu.VMEM((pairs, 2, model // (2 * pairs), block), BF)],
        2 * length * model * total,
        length * (model + total) * 2 + model * total * 2,
        (parity, *lefts, *rights),
    )


def make_body(dp, group):
    pairs = dp // 2
    swap = [(i, i ^ 1) for i in range(dp)]
    lines = [list(range(0, dp, 2)), list(range(1, dp, 2))]
    over_core = [(i, i ^ 1) for i in range(group)]
    over_x = [(i, i ^ 2) for i in range(group)]

    def body(
        tokens,
        context,
        positions,
        seq_mask,
        cotangent,
        norm_gains,
        norm_shifts,
        w_qkv,
        w_self_out,
        w_cross_q,
        w_cross_kv,
        w_cross_out,
        w_gate_up,
        w_down,
    ):
        PAIRS["pairs"] = pairs
        rank = lax.axis_index("dp")
        spot = lax.axis_index("tensor")
        parity = (rank % 2).astype(jnp.int32).reshape(1)
        seqs, part_rows, model = tokens.shape
        length = positions.shape[1]
        ctx_len = context.shape[1]
        rows = w_qkv.shape[1]
        width = w_qkv.shape[2]
        heads = width // HEAD_WIDTH
        hidden = w_down.shape[0]
        ctx_rows = w_cross_kv.shape[1]

        turns = {}

        def in_turn(axis, v, pairs_of, name):
            if axis in turns:
                v = after(v, turns[axis])
            turns[axis] = lax.ppermute(v, name, pairs_of)
            return turns[axis]

        def fetch_all(local):
            return lax.all_gather(local, "dp", axis=0, tiled=True)

        def pair_sum(own, other, *ready):
            got = in_turn("y", other, swap, "dp")
            return own + after(got, *ready)

        def line_sum(v):
            return lax.psum_scatter(v, "dp", scatter_dimension=0, tiled=True, axis_index_groups=lines).astype(F32)

        def core(v):
            return lax.ppermute(v, "tensor", over_core)

        def across(v):
            return in_turn("x", v, over_x, "tensor")

        def spread(own):
            far = across(own)
            return (own, far, core(own), core(far))

        def reduce_rows(keep, send):
            got = core(send)
            far = (keep[part_rows:].astype(F32) + got[part_rows:].astype(F32)).astype(BF)
            return keep, got, across(far)

        def gather_sum(keep, got, back):
            return keep[:part_rows].astype(F32) + got[:part_rows].astype(F32) + back.astype(F32)

        def reduce_parts(own, far, near, both):
            own = (own.astype(F32) + core(near).astype(F32)).astype(BF)
            far = (far.astype(F32) + core(both).astype(F32)).astype(BF)
            return own, across(far)

        def total_of(v):
            v = v + lax.ppermute(v, "tensor", over_core)
            for bit in range((dp - 1).bit_length()):
                v = v + lax.ppermute(v, "dp", [(i, i ^ (1 << bit)) for i in range(dp)])
            return v + across(v)

        order = jnp.stack([spot, spot ^ 2, spot ^ 1, spot ^ 3])
        half_rot = ROT // 2
        lane = jnp.arange(2 * HEAD_WIDTH) % HEAD_WIDTH
        inverse = jnp.exp((lane % half_rot).astype(F32) * (-2.0 * math.log(10000.0) / ROT))
        tables = []
        for s in range(seqs):
            spots = jnp.take(positions[s].reshape(group, part_rows), order, axis=0).reshape(length)
            angles = spots.astype(F32)[:, None] * inverse[None, :]
            turned = lane < ROT
            sine = jnp.sin(angles)
            tables.append(
                (
                    jnp.where(turned, jnp.cos(angles), 1.0),
                    jnp.where(lane < half_rot, sine, 0.0),
                    jnp.where((lane >= half_rot) & turned, sine, 0.0),
                )
            )

        place = rank * group + spot
        mine = jnp.concatenate([norm_gains, norm_shifts], axis=0)
        share = mine.shape[1]
        token_parts = spread(tokens)
        norms = total_of(lax.dynamic_update_slice(jnp.zeros((6, model), F32), mine, (0, place * share)))
        gains = [norms[j : j + 1] for j in range(3)]
        shifts = [norms[3 + j : 4 + j] for j in range(3)]
        keep_scale = seq_mask.astype(F32)[:, None, None]
        grad_third = cotangent.astype(F32) * keep_scale
        third_parts = spread(grad_third.astype(BF))

        w_one = jnp.transpose(w_qkv, (1, 0, 2)).reshape(rows, 3 * width)
        qkv_full = fetch_all(w_one)
        w_two = jnp.concatenate(
            [w_cross_q, w_cross_out.T, w_self_out.T, w_cross_kv.reshape(rows, width)], axis=1
        )
        two_full = fetch_all(after(w_two, qkv_full, token_parts[1], tables[0][0], norms))

        state = [dict() for _ in range(seqs)]
        for s in range(seqs):
            st = state[s]
            gain = gains[0]
            if s > 0:
                gain = after(gain, state[0]["att"], third_parts[1])
            st["normed1"], st["q"], st["k"], st["v"], st["att"], st["lse"] = self_forward(
                token_parts, s, gain, shifts[0], qkv_full, *tables[s], heads
            )
        last = state[seqs - 1]["att"]
        two_full = after(two_full, last)
        gu_full = lax.all_gather(after(w_gate_up, two_full), "dp", axis=1, tiled=True)
        cross_parts = spread(two_full[:, : 2 * width])

        ctx_pad = -(-ctx_len // 128) * 128
        kv_weight = jnp.transpose(two_full[:, 3 * width :].reshape(dp, 2, ctx_rows, width), (1, 0, 2, 3))
        kv_weight = kv_weight.reshape(2, dp * ctx_rows, width)
        cross_kv = jnp.einsum("scd,kdh->skch", context, kv_weight, preferred_element_type=F32).astype(BF)
        cross_kv = jnp.stack(spread(cross_kv))
        cross_kv = jnp.pad(cross_kv, ((0, 0), (0, 0), (0, 0), (0, ctx_pad - ctx_len), (0, 0)))

        for s in range(seqs):
            st = state[s]
            st["terms"] = reduce_rows(*project(after(st["att"], last), two_full, 2))
            last = st["terms"][0]
        for s in range(seqs):
            st = state[s]
            terms = st["terms"]
            if s > 0:
                terms = (after(terms[0], state[s - 1]["second"]), *terms[1:])
            st["first"], st["second"], st["normed2"], normed3, st["cq"], st["crossed"], st["clse"] = cross_forward(
                tokens, s, terms, norms, cross_parts, cross_kv, ctx_len
            )
            st["normed3"] = spread(normed3)
        dn_full = fetch_all(after(w_down.T, gu_full, *(st["normed3"][0] for st in state)))
        for s in range(seqs):
            st = state[s]
            st["gate"], st["up"], st["hidden"] = gate_forward(st["normed3"], gu_full)
        third_lefts = [part[s] for s in range(seqs) for part in third_parts]
        dn_pair = weight_grad(parity, third_lefts, [st["hidden"] for st in state], 512)
        last = dn_pair[1]
        for s in range(seqs):
            st = state[s]
            st["dgate"], st["dup"], keep, send = gate_backward(
                third_parts, s, after(st["gate"], last), st["up"], dn_full, gu_full
            )
            last = keep
            st["d_normed3"] = reduce_rows(keep, send)
        dn_sum = pair_sum(*dn_pair, last)
        dn_grad = line_sum(dn_sum)
        normed3 = [p for st in state for p in st["normed3"]]
        gate_pair = weight_grad(parity, normed3, [after(st["dgate"], dn_sum) for st in state], 512)
        up_pair = weight_grad(parity, normed3, [after(st["dup"], gate_pair[1]) for st in state], 512)

        gain_grads, shift_grads = [0.0] * 3, [0.0] * 3
        last = up_pair[1]
        for s in range(seqs):
            st = state[s]
            st["d_first"], st["dy2"], dy1, st["dcq"], st["dkv"], stats = cross_backward(
                third_parts[0], s, st["d_normed3"], st["second"], after(st["first"], last), norms, cross_parts,
                cross_kv, st["cq"], st["crossed"], st["clse"], ctx_len,
            )
            last = dy1
            for j in range(1, 3):
                gain_grads[j] += stats[j - 1]
                shift_grads[j] += stats[j + 1]
            st["dy1"] = spread(dy1)
        gate_sum = pair_sum(*gate_pair, last)
        gate_part = line_sum(after(gate_sum, dn_grad))
        cross_terms = cross_weight_grad(
            parity,
            [after(st["normed2"], last, state[0]["dy1"][1]) for st in state],
            [st["dy2"] for st in state],
            [st["dcq"] for st in state],
            [st["crossed"] for st in state],
            group,
        )
        up_other = after(up_pair[1], last)
        last = cross_terms[0]
        for s in range(seqs):
            st = state[s]
            st["out_terms"] = project(after(st["hidden"], last), dn_full)
            last = st["out_terms"][0]
        dkv_own, dkv_far = reduce_parts(*(jnp.stack([st["dkv"][p] for st in state]) for p in range(group)))
        cross_mine, cross_far = reduce_parts(*cross_terms)
        last = (last, dn_grad, gate_sum, *(p for st in state for p in st["dy1"]))
        for s in range(seqs):
            st = state[s]
            st["dqkv"], keep, send = self_backward(
                st["dy1"], two_full, qkv_full,
                after(st["q"], *last), st["k"], st["v"], st["att"], st["lse"], *tables[s],
            )
            last = keep
            st["d_normed1"] = (keep, send)
            if s > 0:
                continue
            up_sum = pair_sum(up_pair[0], up_other, last)
            up_part = line_sum(after(up_sum, gate_part))
            so_pair = weight_grad(
                parity,
                [p for st in state for p in st["dy1"]],
                [after(st["att"], last, gate_part) for st in state],
                width,
            )
            dkv = (dkv_own.astype(F32) + after(dkv_far, last).astype(F32)).astype(BF)[:, :, :ctx_len]
            kv_grad = jnp.einsum("scd,skch->kdh", context, dkv, preferred_element_type=F32).astype(BF)
            kv_grad = jnp.transpose(kv_grad.reshape(2, pairs, 2, ctx_rows, width), (1, 2, 0, 3, 4))
            even = parity[0] == 0
            kv_mine = jnp.where(even, kv_grad[:, 0], kv_grad[:, 1]).reshape(pairs * rows, width)
            kv_other = jnp.where(even, kv_grad[:, 1], kv_grad[:, 0]).reshape(pairs * rows, width)
            cross_sum = cross_mine + after(cross_far, so_pair)
            middle_pair = [
                jnp.concatenate(v, axis=1)
                for v in ((cross_sum[0], kv_mine, so_pair[0]), (cross_sum[1], kv_other, so_pair[1]))
            ]
            last = (up_sum, *middle_pair)
        middle_sum = pair_sum(*middle_pair, keep)
        normed1 = [st["normed1"] for st in state]
        qkv_pair = weight_grad(
            parity, normed1, [after(st["dqkv"], up_part) for st in state], width
        )
        middle = line_sum(after(middle_sum, up_part))
        for st in state:
            st["out_terms"] = reduce_rows(*st["out_terms"])
        for st in state:
            st["d_normed1"] = reduce_rows(*st["d_normed1"])
        qkv_part = line_sum(after(pair_sum(*qkv_pair, state[0]["d_normed1"][2]), middle))
        outs = []
        for s in range(seqs):
            st = state[s]
            third = st["second"] + gather_sum(*st["out_terms"])
            outs.append((third * keep_scale[s]).astype(BF))
        grad_inputs = []
        for s in range(seqs):
            st = state[s]
            xhat, inv = norm_parts(tokens[s].astype(F32))
            back, gain_term, shift_term = norm_back(
                gather_sum(*(after(v, qkv_pair[1]) for v in st["d_normed1"])), xhat, inv, gains[0]
            )
            gain_grads[0] += gain_term
            shift_grads[0] += shift_term
            grad_inputs.append(st["d_first"] + back)
        norm_grads = lax.dynamic_slice(
            total_of(jnp.stack(gain_grads + shift_grads)), (0, place * share), (6, share)
        )
        return (
            jnp.stack(outs),
            jnp.stack(grad_inputs),
            norm_grads[:3],
            norm_grads[3:],
            jnp.transpose(qkv_part.reshape(rows, 3, width), (1, 0, 2)),
            middle[:, 3 * width :].T,
            middle[:, :width],
            middle[:, 2 * width : 3 * width].reshape(2, ctx_rows, width),
            middle[:, width : 2 * width].T,
            jnp.stack([gate_part, up_part]),
            dn_grad.T,
        )

    return body


def norm_parts(rows):
    mean = jnp.mean(rows, axis=-1, keepdims=True)
    centred = rows - mean
    inv = lax.rsqrt(jnp.mean(centred * centred, axis=-1, keepdims=True) + EPS)
    return centred * inv, inv


def norm_back(grad, xhat, inv, gain):
    scaled = grad * gain
    back = inv * (
        scaled
        - jnp.mean(scaled, axis=-1, keepdims=True)
        - xhat * jnp.mean(scaled * xhat, axis=-1, keepdims=True)
    )
    return back, jnp.sum(grad * xhat, axis=0), jnp.sum(grad, axis=0)


def solution(mesh):
    in_specs = (
        P("dp", "tensor", None),
        P("dp", None, None),
        P("dp", None),
        P("dp"),
        P("dp", "tensor", None),
        P(None, ("dp", "tensor")),
        P(None, ("dp", "tensor")),
        P(None, "dp", "tensor"),
        P("tensor", "dp"),
        P("dp", "tensor"),
        P(None, "dp", "tensor"),
        P("tensor", "dp"),
        P(None, "dp", "tensor"),
        P("tensor", "dp"),
    )
    out_specs = (
        P("dp", "tensor", None),
        P("dp", "tensor", None),
        P(None, ("dp", "tensor")),
        P(None, ("dp", "tensor")),
        P(None, "dp", "tensor"),
        P("tensor", "dp"),
        P("dp", "tensor"),
        P(None, "dp", "tensor"),
        P("tensor", "dp"),
        P(None, "dp", "tensor"),
        P("tensor", "dp"),
    )
    body = make_body(mesh.shape["dp"], mesh.shape["tensor"])
    return jax.shard_map(body, mesh=mesh, in_specs=in_specs, out_specs=out_specs, check_vma=False)
```
